32 devices in a mesh: dp: 2 (over y), head: 2 (over core), tile: 8 (over z, x).
Axes of the slice: x: 2, y: 2, z: 4, core: 2. Of those that a mesh axis runs over, the one named last changes fastest.
Arguments:
- tiles_in: bfloat16 [2, 2048, 2560], P('dp', 'tile'), may hold values from -6 to 6
- key_weight: bfloat16 [2560, 1280], P('tile', 'head'), may hold values from -0.125 to 0.125
- value_weight: bfloat16 [2560, 1280], P('tile', 'head'), may hold values from -0.125 to 0.125
- queries: bfloat16 [512, 1280], P(None, 'head'), may hold values from -300 to 300
- out_grad: bfloat16 [2, 512, 1280], P('dp', None, 'head'), may hold values from -192 to 192
- valid_count: int32 [2], P('dp'), may hold values from 512 to 2048, as said below
- tile_mask: int32 [2, 2048], P('dp', 'tile'), may hold values 0 or 1
Outputs:
- tile_grad: bfloat16 [2, 2048, 2560], P('dp', 'tile', 'head')
The draws below stay inside these ranges and needn't reach their ends.
Inputs may be any that keep to these rules, and one draw needn't show every extreme that they name: Some slide has valid_count equal to 2048.
All inputs are finite; a program needn't handle non-finite values. No bound on the sum of `tile_mask` on one device may be relied on, other than what follows from the above.
Results may differ from the reference program's by a relative error of at most 0.022.
Values may be sent and summed in bfloat16 or wider, within the bound.
A program may use at most 64 MiB of HBM per device.

```python
import jax
import jax.numpy as jnp
from jax import lax

L = 512
HEADS = 16
HDIM = 80
DX = 2560
TILES = 2048
SLIDES = 2
HD = 1280
N_HEAD = 2


def draw_queries(key, part):
    base = jnp.clip(jax.random.normal(key, (L, HD), jnp.float32), -5.0, 5.0)
    return base.astype(jnp.bfloat16)


def draw_valid_count(key, part):
    first_key = jax.random.fold_in(key, 11)
    second_key = jax.random.fold_in(key, 23)
    counts = jax.random.randint(first_key, (SLIDES,), TILES // 4, TILES + 1, dtype=jnp.int32)
    chosen = jax.random.randint(second_key, (), 0, SLIDES, dtype=jnp.int32)
    return jnp.where(jnp.arange(SLIDES, dtype=jnp.int32) == chosen, jnp.int32(TILES), counts)


def touch_ends(array, rng, smallest, largest):
    shape = array.shape
    index_at = [jax.random.randint(jax.random.fold_in(rng, axis), (), 0, shape[axis]) for axis in range(len(shape))]
    array = array.at[tuple(index_at)].set(smallest)
    longest = shape.index(max(shape))
    index_at[longest] = (index_at[longest] + 1) % shape[longest]
    return array.at[tuple(index_at)].set(largest)


def steps_of(rng, dims, split, least, largest):
    loudness = 1.0
    for dim, blocks in split:
        draws = jax.random.uniform(jax.random.fold_in(jax.random.fold_in(rng, 6), dim), (blocks,), jnp.float32, least / len(split), largest / len(split))
        loudness = loudness * jnp.repeat(jnp.exp(draws), dims[dim] // blocks).reshape((-1,) + (1,) * (len(dims) - 1 - dim))
    return loudness


def normal_values(rng, extent, width, most, cuts=(), held_as=jnp.bfloat16):
    values = width * jax.random.normal(rng, extent, jnp.float32)
    if cuts:
        values = values * steps_of(rng, extent, cuts, -0.22, 0.18)
    return jnp.clip(values, -most, most).astype(held_as)


def setup_inputs(seed: int = 0) -> dict:
    arg_keys = jax.random.split(jax.random.key(seed), 8)
    return {
        "tiles_in": normal_values(arg_keys[0], (SLIDES, TILES, DX), 1.0, 6.0, ((0, 2), (1, 8))),
        "key_weight": normal_values(arg_keys[1], (DX, HD), DX ** -0.5, 0.125, ((0, 8), (1, 2))),
        "value_weight": normal_values(arg_keys[2], (DX, HD), DX ** -0.5, 0.125, ((0, 8), (1, 2))),
        "queries": draw_queries(jax.random.fold_in(arg_keys[7], 71), 0),
        "out_grad": normal_values(arg_keys[4], (SLIDES, L, HD), (TILES / 64), 192.0, ((0, 2), (2, 2))),
        "valid_count": draw_valid_count(jax.random.fold_in(arg_keys[7], 71), 0),
        "tile_mask": touch_ends((jax.random.randint(arg_keys[6], (SLIDES, TILES), 0, 8) < 7).astype(jnp.int32), jax.random.fold_in(arg_keys[6], 1), 0, 1),
    }


NEG_LARGE = -1e30


def one_slide(tiles_one, grad_one, count_one, mask_one, key_weight, value_weight, queries):
    inv_scale = HDIM ** -0.5
    keys = jnp.dot(tiles_one, key_weight, preferred_element_type=jnp.float32)
    values = jnp.dot(tiles_one, value_weight, preferred_element_type=jnp.float32).astype(jnp.bfloat16)
    positions = jnp.arange(TILES, dtype=jnp.int32)
    valid = ((positions < count_one) & ((mask_one == 1) | (positions == 0)))[None, :]
    queries_wide = queries.astype(jnp.float32)

    def one_head(head_index):
        first = (head_index * HDIM).astype(jnp.int32)
        zero = jnp.zeros((), jnp.int32)
        query_cols = lax.dynamic_slice(queries, (zero, first), (L, HDIM))
        query_wide = lax.dynamic_slice(queries_wide, (zero, first), (L, HDIM))
        key_cols = lax.dynamic_slice(keys, (zero, first), (TILES, HDIM))
        value_cols = lax.dynamic_slice(values, (zero, first), (TILES, HDIM))
        grad_cols = lax.dynamic_slice(grad_one, (zero, first), (L, HDIM))
        scores = jnp.dot(query_wide, key_cols.T, precision=lax.Precision.HIGHEST, preferred_element_type=jnp.float32) * inv_scale
        row_max = jnp.max(jnp.where(valid, scores, NEG_LARGE), axis=1)
        expd = jnp.where(valid, jnp.exp(scores - row_max[:, None]), 0.0)
        total = jnp.sum(expd, axis=1)
        prob_grad = jnp.dot(grad_cols, value_cols.T, preferred_element_type=jnp.float32)
        delta = jnp.sum(expd * prob_grad, axis=1) / total
        probs = expd / total[:, None]
        dscore = (inv_scale * probs * (prob_grad - delta[:, None])).astype(jnp.bfloat16)
        value_grad = jnp.dot(probs.astype(jnp.bfloat16).T, grad_cols, preferred_element_type=jnp.float32).astype(jnp.bfloat16)
        key_grad = jnp.dot(dscore.T, query_cols, preferred_element_type=jnp.float32).astype(jnp.bfloat16)
        return key_grad, value_grad

    key_grad, value_grad = lax.map(one_head, jnp.arange(HEADS, dtype=jnp.int32))
    key_grad = jnp.transpose(key_grad, (1, 0, 2)).reshape(TILES, HD)
    value_grad = jnp.transpose(value_grad, (1, 0, 2)).reshape(TILES, HD)
    group_width = HD // N_HEAD
    summed = jnp.zeros((TILES, DX), jnp.float32)
    for group in range(N_HEAD):
        lower = group * group_width
        upper = lower + group_width
        partial_sum = jnp.dot(key_grad[:, lower:upper], key_weight[:, lower:upper].T, preferred_element_type=jnp.float32)
        partial_sum = partial_sum + jnp.dot(value_grad[:, lower:upper], value_weight[:, lower:upper].T, preferred_element_type=jnp.float32)
        rounded = lax.optimization_barrier(partial_sum.astype(jnp.bfloat16))
        summed = summed + rounded.astype(jnp.float32)
    return summed.astype(jnp.bfloat16)


def reference(tiles_in, key_weight, value_weight, queries, out_grad, valid_count, tile_mask):
    results = []
    for slide in range(SLIDES):
        results.append(one_slide(tiles_in[slide], out_grad[slide], valid_count[slide], tile_mask[slide], key_weight, value_weight, queries))
    return jnp.stack(results, axis=0)
```

```python
import functools

import jax
import jax.numpy as jnp
from jax import lax
from jax.experimental import pallas as pl
from jax.experimental.pallas import tpu as pltpu
from jax.sharding import PartitionSpec as P

HDIM = 80


NEG_LARGE = -1e30
NEG_FLOOR = -1e29
WIN = 256
UP, DOWN, ACROSS, TWIN = range(4)
MESH = pl.DeviceIdType.MESH


def per_device(tiles_in, key_weight, value_weight, queries, out_grad, valid_count, tile_mask):
    inv_scale = HDIM ** (-0.5)
    tile_dev = tiles_in.shape[1]
    group_width = queries.shape[1]
    heads_here = group_width // HDIM
    latents = queries.shape[0]
    local_tiles = tiles_in[0]
    positions = lax.axis_index("tile") * tile_dev + jnp.arange(tile_dev, dtype=jnp.int32)
    kept = (tile_mask[0] == 1) | (positions == 0)
    valid = ((positions < valid_count[0]) & kept)[None, None, :]
    full_key, full_value = (
        lax.all_gather(key_weight, "tile", axis=0, tiled=True),
        lax.all_gather(value_weight, "tile", axis=0, tiled=True),
    )
    keys = jnp.dot(local_tiles, full_key, preferred_element_type=jnp.float32)
    values = jnp.dot(local_tiles, full_value, preferred_element_type=jnp.float32).astype(
        jnp.bfloat16
    )
    query_heads = queries.reshape(latents, heads_here, HDIM)
    query_wide = queries.astype(jnp.float32).reshape(latents, heads_here, HDIM)
    key_heads = keys.reshape(tile_dev, heads_here, HDIM)
    value_heads = values.reshape(tile_dev, heads_here, HDIM)
    grad_heads = out_grad[0].reshape(latents, heads_here, HDIM)
    scores = (
        jnp.einsum(
            "lhd,thd->hlt",
            query_wide,
            key_heads,
            precision=lax.Precision.HIGHEST,
            preferred_element_type=jnp.float32,
        )
        * inv_scale
    )
    prob_grad = jnp.einsum(
        "lhd,thd->hlt", grad_heads, value_heads, preferred_element_type=jnp.float32
    )
    local_max = jnp.max(jnp.where(valid, scores, NEG_LARGE), axis=2)
    row_max = lax.pmax(local_max, "tile")
    expd = jnp.where(valid, jnp.exp(scores - row_max[:, :, None]), 0.0)
    total, weighted = lax.psum((jnp.sum(expd, axis=2), jnp.sum(expd * prob_grad, axis=2)), "tile")
    delta = weighted / total
    probs = expd / total[:, :, None]
    dscore = (inv_scale * probs * (prob_grad - delta[:, :, None])).astype(jnp.bfloat16)
    value_grad = (
        jnp.einsum(
            "hlt,lhd->thd",
            probs.astype(jnp.bfloat16),
            grad_heads,
            preferred_element_type=jnp.float32,
        )
        .astype(jnp.bfloat16)
        .reshape(tile_dev, group_width)
    )
    key_grad = (
        jnp.einsum("hlt,lhd->thd", dscore, query_heads, preferred_element_type=jnp.float32)
        .astype(jnp.bfloat16)
        .reshape(tile_dev, group_width)
    )
    partial_sum = jnp.einsum("tc,rc->tr", key_grad, full_key, preferred_element_type=jnp.float32)
    partial_sum = partial_sum + jnp.einsum(
        "tc,rc->tr", value_grad, full_value, preferred_element_type=jnp.float32
    )
    rounded = partial_sum.astype(jnp.bfloat16)
    summed = lax.psum_scatter(rounded[None], "head", scatter_dimension=2, tiled=True).astype(
        jnp.float32
    )
    return summed.astype(jnp.bfloat16)


def dot_nt(a, b):
    return lax.dot_general(a, b, (((1,), (1,)), ((), ())), preferred_element_type=jnp.float32)


def dot_nn(a, b):
    return jnp.dot(a, b, preferred_element_type=jnp.float32)


def fused(
    line, across, shard, width, heads, chunks,
    tiles_hbm, key_hbm, value_hbm, query_hbm, grad_hbm, valid_ref,
    out_ref,
    weights, tiles, query, grad, query_win, grad_win, key_parts, values, expd, prob_grad,
    max_buf, lse_all, weighted_all, row_buf, value_grad, key_grad, acc, to_pair, from_pair,
    local_sem, send_sem, recv_sem, lse_send, lse_recv, sum_send, sum_recv, pair_send, pair_recv,
):
    n_tile = line * across
    half = shard // 2
    inv_scale = HDIM ** (-0.5)
    me = lax.axis_index("tile")
    slide = lax.axis_index("dp")
    group = lax.axis_index("head")
    z = me // across
    x = me % across
    beside = me + 1 - 2 * x
    twin = slide + 1 - 2 * (slide % 2)
    mine, other = slide % 2, 1 - slide % 2
    devices = {
        UP: {"tile": me + across},
        DOWN: {"tile": me - across},
        ACROSS: {"tile": beside},
        TWIN: {"dp": twin},
    }
    sources = (key_hbm, value_hbm)
    started = []

    def copy_in(src, dst, index):
        copy = pltpu.make_async_copy(src, dst, local_sem.at[index])
        copy.start()
        return copy

    own_rows = pl.ds(pl.multiple_of(me * shard, 16), shard)
    query_copy = copy_in(query_hbm, query, 0)
    grad_copy = copy_in(grad_hbm.at[0], grad, 1)
    tiles_copy = copy_in(tiles_hbm.at[0], tiles, 2)
    own_copies = [copy_in(sources[m], weights.at[m, own_rows], 3 + m) for m in range(2)]

    barrier = pltpu.get_barrier_semaphore()
    for step in range(1, n_tile):
        pl.semaphore_signal(
            barrier, inc=1, device_id={"tile": (me + step) % n_tile}, device_id_type=MESH
        )
    pl.semaphore_signal(barrier, inc=1, device_id={"dp": twin}, device_id_type=MESH)
    pl.semaphore_signal(barrier, inc=1, device_id={"head": 1 - group}, device_id_type=MESH)
    pl.semaphore_wait(barrier, n_tile + 1)

    def piece(m, owner, part, way, first=False):
        rows = pl.ds(pl.multiple_of(owner * shard + part * half, 16), half)
        src = weights.at[m, rows]
        if first:
            src = sources[m].at[pl.ds(pl.multiple_of(part * half, 16), half)]
        index = ((m * n_tile + owner) * 2 + part) * 4 + way
        return pltpu.make_async_remote_copy(
            src_ref=src,
            dst_ref=weights.at[m, rows],
            send_sem=send_sem.at[index],
            recv_sem=recv_sem.at[(m * n_tile + owner) * 2 + part],
            device_id=devices[way],
            device_id_type=MESH,
        )

    def send(cond, *what):
        if cond is None:
            piece(*what).start()
        else:
            pl.when(cond)(lambda: piece(*what).start())
        started.append((cond, what))

    def arrive(cond, m, owner, part):
        if cond is None:
            piece(m, owner, part, ACROSS).wait_recv()
        else:
            pl.when(cond)(lambda: piece(m, owner, part, ACROSS).wait_recv())

    def both(a, b):
        return b if a is None else (a if b is None else jnp.logical_and(a, b))

    can_up, can_down = z < line - 1, z > 0

    def open_round(m):
        send(can_up, m, me, mine, UP, True)
        send(can_down, m, me, mine, DOWN, True)
        send(None, m, me, mine, ACROSS, True)
        send(can_up, m, me, other, UP, True)
        send(can_down, m, me, other, DOWN, True)

    def held_at(base, distance):
        if distance == 0:
            return [(None, base)]
        return [
            (z >= distance, base - distance * across),
            (z + distance < line, base + distance * across),
        ]

    def side_round(m, distance):
        for there, owner in held_at(beside, distance):
            arrive(there, m, owner, mine)
            send(there, m, owner, mine, TWIN)

    def line_round(m, distance):
        last = distance == line - 1
        ways = ((UP, can_up), (DOWN, can_down))
        for (there, owner), (way, can) in zip(held_at(me, distance), ways):
            arrive(there, m, owner, mine)
            if not last:
                send(both(there, can), m, owner, mine, way)
            send(there, m, owner, mine, ACROSS)
            if last:
                send(there, m, owner, mine, TWIN)
        if not last:
            for (there, owner), (way, can) in zip(held_at(me, distance), ways):
                arrive(there, m, owner, other)
                if distance + 1 < line - 1:
                    send(both(there, can), m, owner, other, way)
        side_round(m, distance - 1)

    def close_round(m):
        side_round(m, line - 1)
        for distance in range(line):
            for there, owner in held_at(beside, distance):
                arrive(there, m, owner, other)
        for there, owner in held_at(me, line - 1):
            arrive(there, m, owner, other)

    def window(head):
        start = 128 * jnp.minimum((head * HDIM) // 128, (width - WIN) // 128)
        return pl.multiple_of(start, 128)

    def spread(buffer, send_sems, recv_sems):
        copies = []
        for step in range(1, n_tile):
            copies.append(
                pltpu.make_async_remote_copy(
                    src_ref=buffer.at[me],
                    dst_ref=buffer.at[me],
                    send_sem=send_sems.at[step],
                    recv_sem=recv_sems.at[me],
                    device_id={"tile": (me + step) % n_tile},
                    device_id_type=MESH,
                )
            )
            copies[-1].start()
        return copies

    def collect(buffer, send_sems, recv_sems):
        for step in range(1, n_tile):
            owner = (me + n_tile - step) % n_tile
            pltpu.make_async_remote_copy(
                src_ref=buffer.at[owner],
                dst_ref=buffer.at[owner],
                send_sem=send_sems.at[step],
                recv_sem=recv_sems.at[owner],
                device_id={"tile": owner},
                device_id_type=MESH,
            ).wait_recv()

    open_round(0)

    query_copy.wait()
    grad_copy.wait()

    @pl.loop(0, heads)
    def _(head):
        start = window(head)
        column = start + lax.broadcasted_iota(jnp.int32, (query.shape[0], WIN), 1)
        inside = (column >= head * HDIM) & (column < (head + 1) * HDIM)
        for whole, cut in ((query, query_win), (grad, grad_win)):
            part = whole[:, pl.ds(start, WIN)].astype(jnp.float32)
            cut[head] = jnp.where(inside, part, 0.0).astype(jnp.bfloat16)

    value_grad[...] = jnp.zeros_like(value_grad)
    key_grad[...] = jnp.zeros_like(key_grad)

    line_round(0, 1)
    for distance in range(2, line):
        line_round(0, distance)
        if distance == 2:
            open_round(1)
    close_round(0)

    tiles_copy.wait()
    for copy in own_copies:
        copy.wait()
    keys = dot_nn(tiles[...], weights[0])
    for index in range(3):
        part = keys.astype(jnp.bfloat16)
        key_parts[index] = part
        keys = keys - part.astype(jnp.float32)

    line_round(1, 1)

    @pl.loop(0, heads)
    def _(head):
        start = window(head)
        cut = query_win[head]
        scores = dot_nt(key_parts[2, :, pl.ds(start, WIN)], cut)
        scores = scores + dot_nt(key_parts[1, :, pl.ds(start, WIN)], cut)
        scores = scores + dot_nt(key_parts[0, :, pl.ds(start, WIN)], cut)
        scores = jnp.where(valid_ref[...] > 0.0, scores * inv_scale, NEG_LARGE)
        row_max = jnp.maximum(jnp.max(scores, axis=0, keepdims=True), NEG_FLOOR)
        powers = jnp.exp(scores - row_max)
        total = jnp.sum(powers, axis=0, keepdims=True)
        expd[head] = powers
        max_buf[pl.ds(head, 1), :] = row_max
        lse_all[me, pl.ds(head, 1), :] = row_max + jnp.log(jnp.maximum(total, 1e-37))

    lse_copies = spread(lse_all, lse_send, lse_recv)
    for distance in range(2, line):
        line_round(1, distance)
    collect(lse_all, lse_send, lse_recv)
    top = lse_all[0]
    for index in range(1, n_tile):
        top = jnp.maximum(top, lse_all[index])
    total = jnp.exp(lse_all[0] - top)
    for index in range(1, n_tile):
        total = total + jnp.exp(lse_all[index] - top)
    row_buf[...] = jnp.exp(max_buf[...] - (top + jnp.log(total)))

    @pl.loop(0, heads)
    def _(head):
        expd[head] = expd[head] * row_buf[pl.ds(head, 1), :]

    @pl.loop(0, heads)
    def _(head):
        start = window(head)
        value_grad[:, pl.ds(start, WIN)] += dot_nn(expd[head].astype(jnp.bfloat16), grad_win[head])

    close_round(1)

    values[...] = dot_nn(tiles[...], weights[1]).astype(jnp.bfloat16)

    @pl.loop(0, heads)
    def _(head):
        start = window(head)
        part = dot_nt(values[:, pl.ds(start, WIN)], grad_win[head])
        prob_grad[head] = part
        weighted_all[me, pl.ds(head, 1), :] = jnp.sum(expd[head] * part, axis=0, keepdims=True)

    sum_copies = spread(weighted_all, sum_send, sum_recv)

    value_cast = value_grad[...].astype(jnp.bfloat16)

    @pl.loop(0, 2 * chunks)
    def _(index):
        rows = pl.ds(pl.multiple_of(index * WIN, WIN), WIN)
        acc[index] = dot_nt(value_cast, weights[1, rows, :])

    collect(weighted_all, sum_send, sum_recv)
    delta = weighted_all[0]
    for index in range(1, n_tile):
        delta = delta + weighted_all[index]
    row_buf[...] = delta

    @pl.loop(0, heads)
    def _(head):
        start = window(head)
        gap = prob_grad[head] - row_buf[pl.ds(head, 1), :]
        dscore = (inv_scale * expd[head] * gap).astype(jnp.bfloat16)
        key_grad[:, pl.ds(start, WIN)] += dot_nn(dscore, query_win[head])

    key_cast = key_grad[...].astype(jnp.bfloat16)

    def pair_copy(index):
        return pltpu.make_async_remote_copy(
            src_ref=to_pair.at[index],
            dst_ref=from_pair.at[index],
            send_sem=pair_send.at[index],
            recv_sem=pair_recv.at[index],
            device_id={"head": 1 - group},
            device_id_type=MESH,
        )

    @pl.loop(0, chunks)
    def _(index):
        chunk = chunks * (1 - group) + index
        rows = pl.ds(pl.multiple_of(chunk * WIN, WIN), WIN)
        to_pair[index] = (acc[chunk] + dot_nt(key_cast, weights[0, rows, :])).astype(jnp.bfloat16)
        pair_copy(index).start()

    @pl.loop(0, chunks)
    def _(index):
        chunk = chunks * group + index
        rows = pl.ds(pl.multiple_of(chunk * WIN, WIN), WIN)
        acc[chunk] += dot_nt(key_cast, weights[0, rows, :])

    for index in range(chunks):
        pair_copy(index).wait_recv()
        total = acc[chunks * group + index] + from_pair[index].astype(jnp.float32)
        out_ref[0, :, index * WIN : (index + 1) * WIN] = total.astype(jnp.bfloat16)

    for index in range(chunks):
        pair_copy(index).wait_send()
    for copy in lse_copies + sum_copies:
        copy.wait_send()
    for cond, what in started:
        if cond is None:
            piece(*what).wait_send()
        else:
            pl.when(cond)(functools.partial(lambda w: piece(*w).wait_send(), what))


def fused_device(across, tiles_in, key_weight, value_weight, queries, out_grad, valid_count, tile_mask):
    n_tile = lax.axis_size("tile")
    tile_dev, depth = tiles_in.shape[1:]
    latents, width = queries.shape
    shard = key_weight.shape[0]
    heads = width // HDIM
    chunks = depth // 2 // WIN
    positions = lax.axis_index("tile") * tile_dev + jnp.arange(tile_dev, dtype=jnp.int32)
    kept = (tile_mask[0] == 1) | (positions == 0)
    valid = ((positions < valid_count[0]) & kept).astype(jnp.float32)[:, None]
    bf16, f32 = jnp.bfloat16, jnp.float32
    dma = pltpu.SemaphoreType.DMA
    return pl.pallas_call(
        functools.partial(fused, n_tile // across, across, shard, width, heads, chunks),
        out_shape=jax.ShapeDtypeStruct((1, tile_dev, depth // 2), bf16),
        in_specs=[pl.BlockSpec(memory_space=pl.ANY)] * 5
        + [pl.BlockSpec(memory_space=pltpu.VMEM)],
        out_specs=pl.BlockSpec(memory_space=pltpu.VMEM),
        scratch_shapes=[
            pltpu.VMEM((2, depth, width), bf16),
            pltpu.VMEM((tile_dev, depth), bf16),
            pltpu.VMEM((latents, width), bf16),
            pltpu.VMEM((latents, width), bf16),
            pltpu.VMEM((heads, latents, WIN), bf16),
            pltpu.VMEM((heads, latents, WIN), bf16),
            pltpu.VMEM((3, tile_dev, width), bf16),
            pltpu.VMEM((tile_dev, width), bf16),
            pltpu.VMEM((heads, tile_dev, latents), f32),
            pltpu.VMEM((heads, tile_dev, latents), f32),
            pltpu.VMEM((heads, latents), f32),
            pltpu.VMEM((n_tile, heads, latents), f32),
            pltpu.VMEM((n_tile, heads, latents), f32),
            pltpu.VMEM((heads, latents), f32),
            pltpu.VMEM((tile_dev, width), f32),
            pltpu.VMEM((tile_dev, width), f32),
            pltpu.VMEM((2 * chunks, tile_dev, WIN), f32),
            pltpu.VMEM((chunks, tile_dev, WIN), bf16),
            pltpu.VMEM((chunks, tile_dev, WIN), bf16),
            dma((5,)),
            dma((2 * n_tile * 2 * 4,)),
            dma((2 * n_tile * 2,)),
            dma((n_tile,)),
            dma((n_tile,)),
            dma((n_tile,)),
            dma((n_tile,)),
            dma((chunks,)),
            dma((chunks,)),
        ],
        compiler_params=pltpu.CompilerParams(
            collective_id=0, has_side_effects=True, vmem_limit_bytes=56 * 2**20
        ),
        cost_estimate=pl.CostEstimate(
            flops=4 * tile_dev * depth * width * 2, bytes_accessed=8 * 2**20, transcendentals=2**20
        ),
    )(tiles_in, key_weight, value_weight, queries, out_grad, valid)


def solution(mesh):
    across = mesh.shape["dp"]

    def device(tiles_in, key_weight, *rest):
        fits = (
            across == 2
            and mesh.shape["head"] == 2
            and mesh.shape["tile"] >= 3 * across
            and key_weight.shape[0] % 32 == 0
            and tiles_in.shape[2] % (2 * WIN) == 0
        )
        body = functools.partial(fused_device, across) if fits else per_device
        return body(tiles_in, key_weight, *rest)

    return jax.shard_map(
        device,
        mesh=mesh,
        in_specs=(
            P("dp", "tile", None),
            P("tile", "head"),
            P("tile", "head"),
            P(None, "head"),
            P("dp", None, "head"),
            P("dp"),
            P("dp", "tile"),
        ),
        out_specs=P("dp", "tile", "head"),
        check_vma=False,
    )
```

```python
import functools

import jax
import jax.numpy as jnp
from jax import lax
from jax.experimental import pallas as pl
from jax.experimental.pallas import tpu as pltpu
from jax.sharding import PartitionSpec as P

HDIM = 80


NEG_LARGE = -1e30
NEG_FLOOR = -1e29
WIN = 256
SUBS = 2
SENDS = 192
UP, DOWN, ACROSS, TWIN = range(4)
MESH = pl.DeviceIdType.MESH


def per_device(tiles_in, key_weight, value_weight, queries, out_grad, valid_count, tile_mask):
    inv_scale = HDIM ** (-0.5)
    tile_dev = tiles_in.shape[1]
    group_width = queries.shape[1]
    heads_here = group_width // HDIM
    latents = queries.shape[0]
    local_tiles = tiles_in[0]
    positions = lax.axis_index("tile") * tile_dev + jnp.arange(tile_dev, dtype=jnp.int32)
    kept = (tile_mask[0] == 1) | (positions == 0)
    valid = ((positions < valid_count[0]) & kept)[None, None, :]
    full_key, full_value = (
        lax.all_gather(key_weight, "tile", axis=0, tiled=True),
        lax.all_gather(value_weight, "tile", axis=0, tiled=True),
    )
    keys = jnp.dot(local_tiles, full_key, preferred_element_type=jnp.float32)
    values = jnp.dot(local_tiles, full_value, preferred_element_type=jnp.float32).astype(
        jnp.bfloat16
    )
    query_heads = queries.reshape(latents, heads_here, HDIM)
    query_wide = queries.astype(jnp.float32).reshape(latents, heads_here, HDIM)
    key_heads = keys.reshape(tile_dev, heads_here, HDIM)
    value_heads = values.reshape(tile_dev, heads_here, HDIM)
    grad_heads = out_grad[0].reshape(latents, heads_here, HDIM)
    scores = (
        jnp.einsum(
            "lhd,thd->hlt",
            query_wide,
            key_heads,
            precision=lax.Precision.HIGHEST,
            preferred_element_type=jnp.float32,
        )
        * inv_scale
    )
    prob_grad = jnp.einsum(
        "lhd,thd->hlt", grad_heads, value_heads, preferred_element_type=jnp.float32
    )
    local_max = jnp.max(jnp.where(valid, scores, NEG_LARGE), axis=2)
    row_max = lax.pmax(local_max, "tile")
    expd = jnp.where(valid, jnp.exp(scores - row_max[:, :, None]), 0.0)
    total, weighted = lax.psum((jnp.sum(expd, axis=2), jnp.sum(expd * prob_grad, axis=2)), "tile")
    delta = weighted / total
    probs = expd / total[:, :, None]
    dscore = (inv_scale * probs * (prob_grad - delta[:, :, None])).astype(jnp.bfloat16)
    value_grad = (
        jnp.einsum(
            "hlt,lhd->thd",
            probs.astype(jnp.bfloat16),
            grad_heads,
            preferred_element_type=jnp.float32,
        )
        .astype(jnp.bfloat16)
        .reshape(tile_dev, group_width)
    )
    key_grad = (
        jnp.einsum("hlt,lhd->thd", dscore, query_heads, preferred_element_type=jnp.float32)
        .astype(jnp.bfloat16)
        .reshape(tile_dev, group_width)
    )
    partial_sum = jnp.einsum("tc,rc->tr", key_grad, full_key, preferred_element_type=jnp.float32)
    partial_sum = partial_sum + jnp.einsum(
        "tc,rc->tr", value_grad, full_value, preferred_element_type=jnp.float32
    )
    rounded = partial_sum.astype(jnp.bfloat16)
    summed = lax.psum_scatter(rounded[None], "head", scatter_dimension=2, tiled=True).astype(
        jnp.float32
    )
    return summed.astype(jnp.bfloat16)


def dot_nt(a, b):
    return lax.dot_general(a, b, (((1,), (1,)), ((), ())), preferred_element_type=jnp.float32)


def dot_nn(a, b):
    return jnp.dot(a, b, preferred_element_type=jnp.float32)


def fused(
    line, across, shard, width, heads, chunks,
    tiles_hbm, key_hbm, value_hbm, query_hbm, grad_hbm, count_ref, mask_ref,
    own_ref, pair_ref,
    weights, tiles, query, grad, query_win, grad_win, key_parts, values, expd, prob_grad,
    max_buf, lse_all, weighted_all, row_buf, value_grad, key_grad, acc, to_pair, valid,
    local_sem, send_sem, recv_sem, lse_send, lse_recv, sum_send, sum_recv, pair_send, pair_recv,
):
    n_tile = line * across
    half = shard // 2
    size = half // SUBS
    inv_scale = HDIM ** (-0.5)
    me = lax.axis_index("tile")
    slide = lax.axis_index("dp")
    group = lax.axis_index("head")
    z = me // across
    x = me % across
    beside = me + 1 - 2 * x
    twin = slide + 1 - 2 * (slide % 2)
    mine, other = slide % 2, 1 - slide % 2
    devices = {
        UP: {"tile": me + across},
        DOWN: {"tile": me - across},
        ACROSS: {"tile": beside},
        TWIN: {"dp": twin},
    }
    sources = (key_hbm, value_hbm)
    started = []

    def copy_in(src, dst, index):
        copy = pltpu.make_async_copy(src, dst, local_sem.at[index])
        copy.start()
        return copy

    own_rows = pl.ds(pl.multiple_of(me * shard, 16), shard)
    query_copy = copy_in(query_hbm, query, 0)
    grad_copy = copy_in(grad_hbm.at[0], grad, 1)
    tiles_copy = copy_in(tiles_hbm.at[0], tiles, 2)
    own_copies = [copy_in(sources[m], weights.at[m, own_rows], 3 + m) for m in range(2)]

    barrier = pltpu.get_barrier_semaphore()
    for step in range(1, n_tile):
        pl.semaphore_signal(
            barrier, inc=1, device_id={"tile": (me + step) % n_tile}, device_id_type=MESH
        )
    pl.semaphore_signal(barrier, inc=1, device_id={"dp": twin}, device_id_type=MESH)
    pl.semaphore_signal(barrier, inc=1, device_id={"head": 1 - group}, device_id_type=MESH)
    pl.semaphore_wait(barrier, n_tile + 1)

    def piece(m, owner, part, sub, way, first=False):
        offset = part * half + sub * size
        rows = pl.ds(pl.multiple_of(owner * shard + offset, 16), size)
        src = weights.at[m, rows]
        if first:
            src = sources[m].at[pl.ds(pl.multiple_of(offset, 16), size)]
        return src, weights.at[m, rows], ((m * n_tile + owner) * 2 + part) * SUBS + sub, devices[way]

    def remote(index, *what):
        src, dst, landing, device = piece(*what)
        return pltpu.make_async_remote_copy(
            src_ref=src,
            dst_ref=dst,
            send_sem=send_sem.at[index],
            recv_sem=recv_sem.at[landing],
            device_id=device,
            device_id_type=MESH,
        )

    def send(cond, *what):
        index = len(started)
        started.append((cond, what))
        if cond is None:
            remote(index, *what).start()
        else:
            pl.when(cond)(lambda: remote(index, *what).start())

    def arrive(cond, m, owner, part, sub):
        if cond is None:
            remote(0, m, owner, part, sub, ACROSS).wait_recv()
        else:
            pl.when(cond)(lambda: remote(0, m, owner, part, sub, ACROSS).wait_recv())

    def both(a, b):
        return b if a is None else (a if b is None else jnp.logical_and(a, b))

    can_up, can_down = z < line - 1, z > 0
    ways = ((UP, can_up), (DOWN, can_down))

    def held_at(base, distance):
        if distance == 0:
            return [(None, base)]
        return [
            (z >= distance, base - distance * across),
            (z + distance < line, base + distance * across),
        ]

    def open_own(m):
        for sub in range(SUBS):
            for way, can in ways:
                send(can, m, me, mine, sub, way, True)
            send(None, m, me, mine, sub, ACROSS, True)

    def side_round(m, distance):
        for sub in range(SUBS):
            for there, owner in held_at(beside, distance):
                arrive(there, m, owner, mine, sub)
                send(there, m, owner, mine, sub, TWIN)

    def own_round(m, distance):
        last = distance == line - 1
        for sub in range(SUBS):
            for (there, owner), (way, can) in zip(held_at(me, distance), ways):
                arrive(there, m, owner, mine, sub)
                if not last:
                    send(both(there, can), m, owner, mine, sub, way)
                send(there, m, owner, mine, sub, ACROSS)
                if last:
                    send(there, m, owner, mine, sub, TWIN)
        for way, can, ends in ((UP, can_up, z), (DOWN, can_down, line - 1 - z)):
            turn = jnp.maximum(ends, 1) == distance
            for sub in range(SUBS):
                send(both(turn, can), m, me, other, sub, way, True)
        side_round(m, distance - 1)

    def other_round(m, distance):
        for sub in range(SUBS):
            for (there, owner), (way, can) in zip(held_at(me, distance), ways):
                arrive(there, m, owner, other, sub)
                if distance + 1 < line - 1:
                    send(both(there, can), m, owner, other, sub, way)

    def close_round(m):
        for sub in range(SUBS):
            for distance in range(line):
                for there, owner in held_at(beside, distance):
                    arrive(there, m, owner, other, sub)
            for there, owner in held_at(me, line - 1):
                arrive(there, m, owner, other, sub)

    def window(head):
        start = 128 * jnp.minimum((head * HDIM) // 128, (width - WIN) // 128)
        return pl.multiple_of(start, 128)

    def spread(buffer, send_sems, recv_sems):
        copies = []
        for step in range(1, n_tile):
            copies.append(
                pltpu.make_async_remote_copy(
                    src_ref=buffer.at[me],
                    dst_ref=buffer.at[me],
                    send_sem=send_sems.at[step],
                    recv_sem=recv_sems.at[me],
                    device_id={"tile": (me + step) % n_tile},
                    device_id_type=MESH,
                )
            )
            copies[-1].start()
        return copies

    def collect(buffer, send_sems, recv_sems):
        for step in range(1, n_tile):
            owner = (me + n_tile - step) % n_tile
            pltpu.make_async_remote_copy(
                src_ref=buffer.at[owner],
                dst_ref=buffer.at[owner],
                send_sem=send_sems.at[step],
                recv_sem=recv_sems.at[owner],
                device_id={"tile": owner},
                device_id_type=MESH,
            ).wait_recv()

    open_own(0)

    positions = me * tiles.shape[0] + lax.broadcasted_iota(jnp.int32, (128, tiles.shape[0]), 1)
    kept = (mask_ref[...] == 1) | (positions == 0)
    valid[...] = jnp.where(kept & (positions < count_ref[0]), 1.0, 0.0).T

    query_copy.wait()
    grad_copy.wait()

    @pl.loop(0, heads)
    def _(head):
        start = window(head)
        column = start + lax.broadcasted_iota(jnp.int32, (query.shape[0], WIN), 1)
        inside = (column >= head * HDIM) & (column < (head + 1) * HDIM)
        for whole, cut in ((query, query_win), (grad, grad_win)):
            part = whole[:, pl.ds(start, WIN)].astype(jnp.float32)
            cut[head] = jnp.where(inside, part, 0.0).astype(jnp.bfloat16)

    value_grad[...] = jnp.zeros_like(value_grad)
    key_grad[...] = jnp.zeros_like(key_grad)

    for distance in range(1, line):
        own_round(0, distance)
    other_round(0, 1)
    side_round(0, line - 1)
    open_own(1)
    for distance in range(2, line - 1):
        other_round(0, distance)
    close_round(0)

    tiles_copy.wait()
    for copy in own_copies:
        copy.wait()
    keys = dot_nn(tiles[...], weights[0])
    for index in range(3):
        part = keys.astype(jnp.bfloat16)
        key_parts[index] = part
        keys = keys - part.astype(jnp.float32)

    def score(first, last):
        @pl.loop(first, last, unroll=2)
        def _(head):
            start = window(head)
            cut = query_win[head]
            scores = dot_nt(key_parts[2, :, pl.ds(start, WIN)], cut)
            scores = scores + dot_nt(key_parts[1, :, pl.ds(start, WIN)], cut)
            scores = scores + dot_nt(key_parts[0, :, pl.ds(start, WIN)], cut)
            scores = jnp.where(valid[:, :1] > 0.0, scores * inv_scale, NEG_LARGE)
            row_max = jnp.maximum(jnp.max(scores, axis=0, keepdims=True), NEG_FLOOR)
            powers = jnp.exp(scores - row_max)
            total = jnp.sum(powers, axis=0, keepdims=True)
            expd[head] = powers
            max_buf[pl.ds(head, 1), :] = row_max
            lse_all[me, pl.ds(head, 1), :] = row_max + jnp.log(jnp.maximum(total, 1e-37))

    cuts = [heads * step // 4 for step in range(5)]
    score(cuts[0], cuts[1])
    own_round(1, 1)
    score(cuts[1], cuts[2])
    own_round(1, 2)
    score(cuts[2], cuts[4])
    lse_copies = spread(lse_all, lse_send, lse_recv)
    for distance in range(3, line):
        own_round(1, distance)
    other_round(1, 1)
    side_round(1, line - 1)
    collect(lse_all, lse_send, lse_recv)
    top = lse_all[0]
    for index in range(1, n_tile):
        top = jnp.maximum(top, lse_all[index])
    total = jnp.exp(lse_all[0] - top)
    for index in range(1, n_tile):
        total = total + jnp.exp(lse_all[index] - top)
    row_buf[...] = jnp.exp(max_buf[...] - (top + jnp.log(total)))

    @pl.loop(0, heads, unroll=2)
    def _(head):
        start = window(head)
        probs = expd[head] * row_buf[pl.ds(head, 1), :]
        expd[head] = probs
        value_grad[:, pl.ds(start, WIN)] += dot_nn(probs.astype(jnp.bfloat16), grad_win[head])

    for distance in range(2, line - 1):
        other_round(1, distance)
    close_round(1)

    values[...] = dot_nn(tiles[...], weights[1]).astype(jnp.bfloat16)

    @pl.loop(0, heads, unroll=2)
    def _(head):
        start = window(head)
        part = dot_nt(values[:, pl.ds(start, WIN)], grad_win[head])
        prob_grad[head] = part
        weighted_all[me, pl.ds(head, 1), :] = jnp.sum(expd[head] * part, axis=0, keepdims=True)

    sum_copies = spread(weighted_all, sum_send, sum_recv)

    value_cast = value_grad[...].astype(jnp.bfloat16)

    @pl.loop(0, 2 * chunks, unroll=2)
    def _(index):
        rows = pl.ds(pl.multiple_of(index * WIN, WIN), WIN)
        acc[index] = dot_nt(value_cast, weights[1, rows, :])

    collect(weighted_all, sum_send, sum_recv)
    delta = weighted_all[0]
    for index in range(1, n_tile):
        delta = delta + weighted_all[index]
    row_buf[...] = delta

    @pl.loop(0, heads, unroll=2)
    def _(head):
        start = window(head)
        gap = prob_grad[head] - row_buf[pl.ds(head, 1), :]
        dscore = (inv_scale * expd[head] * gap).astype(jnp.bfloat16)
        key_grad[:, pl.ds(start, WIN)] += dot_nn(dscore, query_win[head])

    key_cast = key_grad[...].astype(jnp.bfloat16)

    def pair_copy(index):
        columns = pl.ds(index * WIN, WIN)
        return pltpu.make_async_remote_copy(
            src_ref=to_pair.at[:, columns],
            dst_ref=pair_ref.at[:, columns],
            send_sem=pair_send.at[index],
            recv_sem=pair_recv.at[index],
            device_id={"head": 1 - group},
            device_id_type=MESH,
        )

    def partial_sum(chunk):
        rows = pl.ds(pl.multiple_of(chunk * WIN, WIN), WIN)
        return (acc[chunk] + dot_nt(key_cast, weights[0, rows, :])).astype(jnp.bfloat16)

    for index in range(chunks):
        to_pair[:, index * WIN : (index + 1) * WIN] = partial_sum(chunks * (1 - group) + index)
        pair_copy(index).start()
    for index in range(chunks):
        own_ref[:, index * WIN : (index + 1) * WIN] = partial_sum(chunks * group + index)

    for index in range(chunks):
        pair_copy(index).wait_recv()
    for index in range(chunks):
        pair_copy(index).wait_send()
    for copy in lse_copies + sum_copies:
        copy.wait_send()
    assert len(started) <= SENDS
    for index, (cond, what) in enumerate(started):
        if cond is None:
            remote(index, *what).wait_send()
        else:
            pl.when(cond)(functools.partial(lambda i, w: remote(i, *w).wait_send(), index, what))


def fused_device(across, tiles_in, key_weight, value_weight, queries, out_grad, valid_count, tile_mask):
    n_tile = lax.axis_size("tile")
    tile_dev, depth = tiles_in.shape[1:]
    latents, width = queries.shape
    shard = key_weight.shape[0]
    heads = width // HDIM
    chunks = depth // 2 // WIN
    bf16, f32 = jnp.bfloat16, jnp.float32
    dma = pltpu.SemaphoreType.DMA
    own, pair = pl.pallas_call(
        functools.partial(fused, n_tile // across, across, shard, width, heads, chunks),
        out_shape=[jax.ShapeDtypeStruct((tile_dev, depth // 2), bf16)] * 2,
        in_specs=[pl.BlockSpec(memory_space=pl.ANY)] * 5
        + [pl.BlockSpec(memory_space=pltpu.SMEM), pl.BlockSpec(memory_space=pltpu.VMEM)],
        out_specs=[pl.BlockSpec(memory_space=pltpu.VMEM)] * 2,
        scratch_shapes=[
            pltpu.VMEM((2, depth, width), bf16),
            pltpu.VMEM((tile_dev, depth), bf16),
            pltpu.VMEM((latents, width), bf16),
            pltpu.VMEM((latents, width), bf16),
            pltpu.VMEM((heads, latents, WIN), bf16),
            pltpu.VMEM((heads, latents, WIN), bf16),
            pltpu.VMEM((3, tile_dev, width), bf16),
            pltpu.VMEM((tile_dev, width), bf16),
            pltpu.VMEM((heads, tile_dev, latents), f32),
            pltpu.VMEM((heads, tile_dev, latents), f32),
            pltpu.VMEM((heads, latents), f32),
            pltpu.VMEM((n_tile, heads, latents), f32),
            pltpu.VMEM((n_tile, heads, latents), f32),
            pltpu.VMEM((heads, latents), f32),
            pltpu.VMEM((tile_dev, width), f32),
            pltpu.VMEM((tile_dev, width), f32),
            pltpu.VMEM((2 * chunks, tile_dev, WIN), f32),
            pltpu.VMEM((tile_dev, chunks * WIN), bf16),
            pltpu.VMEM((tile_dev, 128), f32),
            dma((5,)),
            dma((SENDS,)),
            dma((2 * n_tile * 2 * SUBS,)),
            dma((n_tile,)),
            dma((n_tile,)),
            dma((n_tile,)),
            dma((n_tile,)),
            dma((chunks,)),
            dma((chunks,)),
        ],
        compiler_params=pltpu.CompilerParams(
            collective_id=0, has_side_effects=True, vmem_limit_bytes=56 * 2**20
        ),
        cost_estimate=pl.CostEstimate(
            flops=4 * tile_dev * depth * width * 2, bytes_accessed=8 * 2**20, transcendentals=2**20
        ),
    )(tiles_in, key_weight, value_weight, queries, out_grad, valid_count, tile_mask)
    return (own.astype(f32) + pair.astype(f32)).astype(bf16)[None]


def solution(mesh):
    across = mesh.shape["dp"]

    def device(tiles_in, key_weight, *rest):
        fits = (
            across == 2
            and mesh.shape["head"] == 2
            and mesh.shape["tile"] >= 3 * across
            and key_weight.shape[0] % (32 * SUBS) == 0
            and tiles_in.shape[2] % (2 * WIN) == 0
        )
        body = functools.partial(fused_device, across) if fits else per_device
        return body(tiles_in, key_weight, *rest)

    return jax.shard_map(
        device,
        mesh=mesh,
        in_specs=(
            P("dp", "tile", None),
            P("tile", "head"),
            P("tile", "head"),
            P(None, "head"),
            P("dp", None, "head"),
            P("dp"),
            P("dp", "tile"),
        ),
        out_specs=P("dp", "tile", "head"),
        check_vma=False,
    )
```

```python
import functools

import jax
import jax.numpy as jnp
from jax import lax
from jax.experimental import pallas as pl
from jax.experimental.pallas import tpu as pltpu
from jax.sharding import PartitionSpec as P

HDIM = 80


NEG_LARGE = -1e30
NEG_FLOOR = -1e29
WIN = 256
SUBS = 2
SENDS = 256
UP, DOWN, ACROSS, TWIN = range(4)
MESH = pl.DeviceIdType.MESH


def per_device(tiles_in, key_weight, value_weight, queries, out_grad, valid_count, tile_mask):
    inv_scale = HDIM ** (-0.5)
    tile_dev = tiles_in.shape[1]
    group_width = queries.shape[1]
    heads_here = group_width // HDIM
    latents = queries.shape[0]
    local_tiles = tiles_in[0]
    positions = lax.axis_index("tile") * tile_dev + jnp.arange(tile_dev, dtype=jnp.int32)
    kept = (tile_mask[0] == 1) | (positions == 0)
    valid = ((positions < valid_count[0]) & kept)[None, None, :]
    full_key, full_value = (
        lax.all_gather(key_weight, "tile", axis=0, tiled=True),
        lax.all_gather(value_weight, "tile", axis=0, tiled=True),
    )
    keys = jnp.dot(local_tiles, full_key, preferred_element_type=jnp.float32)
    values = jnp.dot(local_tiles, full_value, preferred_element_type=jnp.float32).astype(
        jnp.bfloat16
    )
    query_heads = queries.reshape(latents, heads_here, HDIM)
    query_wide = queries.astype(jnp.float32).reshape(latents, heads_here, HDIM)
    key_heads = keys.reshape(tile_dev, heads_here, HDIM)
    value_heads = values.reshape(tile_dev, heads_here, HDIM)
    grad_heads = out_grad[0].reshape(latents, heads_here, HDIM)
    scores = (
        jnp.einsum(
            "lhd,thd->hlt",
            query_wide,
            key_heads,
            precision=lax.Precision.HIGHEST,
            preferred_element_type=jnp.float32,
        )
        * inv_scale
    )
    prob_grad = jnp.einsum(
        "lhd,thd->hlt", grad_heads, value_heads, preferred_element_type=jnp.float32
    )
    local_max = jnp.max(jnp.where(valid, scores, NEG_LARGE), axis=2)
    row_max = lax.pmax(local_max, "tile")
    expd = jnp.where(valid, jnp.exp(scores - row_max[:, :, None]), 0.0)
    total, weighted = lax.psum((jnp.sum(expd, axis=2), jnp.sum(expd * prob_grad, axis=2)), "tile")
    delta = weighted / total
    probs = expd / total[:, :, None]
    dscore = (inv_scale * probs * (prob_grad - delta[:, :, None])).astype(jnp.bfloat16)
    value_grad = (
        jnp.einsum(
            "hlt,lhd->thd",
            probs.astype(jnp.bfloat16),
            grad_heads,
            preferred_element_type=jnp.float32,
        )
        .astype(jnp.bfloat16)
        .reshape(tile_dev, group_width)
    )
    key_grad = (
        jnp.einsum("hlt,lhd->thd", dscore, query_heads, preferred_element_type=jnp.float32)
        .astype(jnp.bfloat16)
        .reshape(tile_dev, group_width)
    )
    partial_sum = jnp.einsum("tc,rc->tr", key_grad, full_key, preferred_element_type=jnp.float32)
    partial_sum = partial_sum + jnp.einsum(
        "tc,rc->tr", value_grad, full_value, preferred_element_type=jnp.float32
    )
    rounded = partial_sum.astype(jnp.bfloat16)
    summed = lax.psum_scatter(rounded[None], "head", scatter_dimension=2, tiled=True).astype(
        jnp.float32
    )
    return summed.astype(jnp.bfloat16)


def dot_nt(a, b):
    return lax.dot_general(a, b, (((1,), (1,)), ((), ())), preferred_element_type=jnp.float32)


def dot_nn(a, b):
    return jnp.dot(a, b, preferred_element_type=jnp.float32)


def fused(
    line, across, shard, width, heads, chunks,
    tiles_hbm, key_hbm, value_hbm, query_hbm, grad_hbm, count_ref, mask_ref,
    own_ref, pair_ref,
    weights, tiles, query, grad, query_win, grad_win, key_parts, values, expd, prob_grad,
    max_buf, lse_all, weighted_all, row_buf, value_grad, key_grad, acc, to_pair, valid,
    local_sem, send_sem, recv_sem, lse_send, lse_recv, sum_send, sum_recv, pair_send, pair_recv,
):
    n_tile = line * across
    half = shard // 2
    bounds = list(range(0, width, WIN)) + [width]
    cuts_of = [(0, 0, width, SUBS)] + [(1, a, b - a, 1) for a, b in zip(bounds, bounds[1:])]
    members = [
        [head for head in range(heads) if a < (head + 1) * HDIM <= b]
        for a, b in zip(bounds, bounds[1:])
    ]
    groups = len(members)
    inv_scale = HDIM ** (-0.5)
    me = lax.axis_index("tile")
    slide = lax.axis_index("dp")
    group = lax.axis_index("head")
    z = me // across
    x = me % across
    beside = me + 1 - 2 * x
    twin = slide + 1 - 2 * (slide % 2)
    mine, other = slide % 2, 1 - slide % 2
    devices = {
        UP: {"tile": me + across},
        DOWN: {"tile": me - across},
        ACROSS: {"tile": beside},
        TWIN: {"dp": twin},
    }
    sources = (key_hbm, value_hbm)
    started = []

    def copy_in(src, dst, index):
        copy = pltpu.make_async_copy(src, dst, local_sem.at[index])
        copy.start()
        return copy

    own_rows = pl.ds(pl.multiple_of(me * shard, 16), shard)
    query_copy = copy_in(query_hbm, query, 0)
    grad_copy = copy_in(grad_hbm.at[0], grad, 1)
    tiles_copy = copy_in(tiles_hbm.at[0], tiles, 2)
    own_copies = [copy_in(sources[m], weights.at[m, own_rows], 3 + m) for m in range(2)]

    barrier = pltpu.get_barrier_semaphore()
    for step in range(1, n_tile):
        pl.semaphore_signal(
            barrier, inc=1, device_id={"tile": (me + step) % n_tile}, device_id_type=MESH
        )
    pl.semaphore_signal(barrier, inc=1, device_id={"dp": twin}, device_id_type=MESH)
    pl.semaphore_signal(barrier, inc=1, device_id={"head": 1 - group}, device_id_type=MESH)
    pl.semaphore_wait(barrier, n_tile + 1)

    def subs(m):
        return range(cuts_of[m][3])

    def piece(m, owner, part, sub, way, first=False):
        which, column, columns, count = cuts_of[m]
        size = half // count
        offset = part * half + sub * size
        cols = pl.ds(column, columns)
        rows = pl.ds(pl.multiple_of(owner * shard + offset, 16), size)
        src = weights.at[which, rows, cols]
        if first:
            src = sources[which].at[pl.ds(pl.multiple_of(offset, 16), size), cols]
        base = n_tile * 2 * sum(cut[3] for cut in cuts_of[:m])
        landing = base + (owner * 2 + part) * count + sub
        return src, weights.at[which, rows, cols], landing, devices[way]

    def remote(index, *what):
        src, dst, landing, device = piece(*what)
        return pltpu.make_async_remote_copy(
            src_ref=src,
            dst_ref=dst,
            send_sem=send_sem.at[index],
            recv_sem=recv_sem.at[landing],
            device_id=device,
            device_id_type=MESH,
        )

    def send(cond, *what):
        index = len(started)
        started.append((cond, what))
        if cond is None:
            remote(index, *what).start()
        else:
            pl.when(cond)(lambda: remote(index, *what).start())

    def arrive(cond, m, owner, part, sub):
        if cond is None:
            remote(0, m, owner, part, sub, ACROSS).wait_recv()
        else:
            pl.when(cond)(lambda: remote(0, m, owner, part, sub, ACROSS).wait_recv())

    def both(a, b):
        return b if a is None else (a if b is None else jnp.logical_and(a, b))

    can_up, can_down = z < line - 1, z > 0
    ways = ((UP, can_up), (DOWN, can_down))

    def held_at(base, distance):
        if distance == 0:
            return [(None, base)]
        return [
            (z >= distance, base - distance * across),
            (z + distance < line, base + distance * across),
        ]

    def open_own(m):
        for sub in subs(m):
            for way, can in ways:
                send(can, m, me, mine, sub, way, True)
            send(None, m, me, mine, sub, ACROSS, True)

    def side_round(m, distance):
        for sub in subs(m):
            for there, owner in held_at(beside, distance):
                arrive(there, m, owner, mine, sub)
                send(there, m, owner, mine, sub, TWIN)

    def own_round(m, distance):
        last = distance == line - 1
        for sub in subs(m):
            for (there, owner), (way, can) in zip(held_at(me, distance), ways):
                arrive(there, m, owner, mine, sub)
                if not last:
                    send(both(there, can), m, owner, mine, sub, way)
                send(there, m, owner, mine, sub, ACROSS)
                if last:
                    send(there, m, owner, mine, sub, TWIN)
        for way, can, ends in ((UP, can_up, z), (DOWN, can_down, line - 1 - z)):
            turn = jnp.maximum(ends, 1) == distance
            for sub in subs(m) if not last else ():
                send(both(turn, can), m, me, other, sub, way, True)
        side_round(m, distance - 1)

    def other_round(m, distance):
        for sub in subs(m):
            for (there, owner), (way, can) in zip(held_at(me, distance), ways):
                arrive(there, m, owner, other, sub)
                if distance + 1 < line - 1:
                    send(both(there, can), m, owner, other, sub, way)

    def close_round(m):
        for sub in subs(m):
            for distance in range(line):
                for there, owner in held_at(beside, distance):
                    arrive(there, m, owner, other, sub)
            for there, owner in held_at(me, line - 1):
                arrive(there, m, owner, other, sub)

    def window(head):
        start = 128 * jnp.minimum((head * HDIM) // 128, (width - WIN) // 128)
        return pl.multiple_of(start, 128)

    def spread(buffer, send_sems, recv_sems):
        copies = []
        for step in range(1, n_tile):
            copies.append(
                pltpu.make_async_remote_copy(
                    src_ref=buffer.at[me],
                    dst_ref=buffer.at[me],
                    send_sem=send_sems.at[step],
                    recv_sem=recv_sems.at[me],
                    device_id={"tile": (me + step) % n_tile},
                    device_id_type=MESH,
                )
            )
            copies[-1].start()
        return copies

    def collect(buffer, send_sems, recv_sems):
        for step in range(1, n_tile):
            owner = (me + n_tile - step) % n_tile
            pltpu.make_async_remote_copy(
                src_ref=buffer.at[owner],
                dst_ref=buffer.at[owner],
                send_sem=send_sems.at[step],
                recv_sem=recv_sems.at[owner],
                device_id={"tile": owner},
                device_id_type=MESH,
            ).wait_recv()

    open_own(0)

    positions = me * tiles.shape[0] + lax.broadcasted_iota(jnp.int32, (128, tiles.shape[0]), 1)
    kept = (mask_ref[...] == 1) | (positions == 0)
    valid[...] = jnp.where(kept & (positions < count_ref[0]), 1.0, 0.0).T

    query_copy.wait()
    grad_copy.wait()

    @pl.loop(0, heads)
    def _(head):
        start = window(head)
        column = start + lax.broadcasted_iota(jnp.int32, (query.shape[0], WIN), 1)
        inside = (column >= head * HDIM) & (column < (head + 1) * HDIM)
        for whole, cut in ((query, query_win), (grad, grad_win)):
            part = whole[:, pl.ds(start, WIN)].astype(jnp.float32)
            cut[head] = jnp.where(inside, part, 0.0).astype(jnp.bfloat16)

    value_grad[...] = jnp.zeros_like(value_grad)
    key_grad[...] = jnp.zeros_like(key_grad)
    values[...] = jnp.zeros_like(values)
    weighted_all[:, me] = jnp.zeros((groups,) + weighted_all.shape[2:], jnp.float32)

    for distance in range(1, line):
        own_round(0, distance)
    other_round(0, 1)
    side_round(0, line - 1)
    open_own(1)
    for distance in range(2, line - 1):
        other_round(0, distance)
    close_round(0)

    tiles_copy.wait()
    for copy in own_copies:
        copy.wait()
    keys = dot_nn(tiles[...], weights[0])
    for index in range(3):
        part = keys.astype(jnp.bfloat16)
        key_parts[index] = part
        keys = keys - part.astype(jnp.float32)

    def score(first, last):
        @pl.loop(first, last, unroll=2)
        def _(head):
            start = window(head)
            cut = query_win[head]
            scores = dot_nt(key_parts[2, :, pl.ds(start, WIN)], cut)
            scores = scores + dot_nt(key_parts[1, :, pl.ds(start, WIN)], cut)
            scores = scores + dot_nt(key_parts[0, :, pl.ds(start, WIN)], cut)
            scores = jnp.where(valid[:, :1] > 0.0, scores * inv_scale, NEG_LARGE)
            row_max = jnp.maximum(jnp.max(scores, axis=0, keepdims=True), NEG_FLOOR)
            powers = jnp.exp(scores - row_max)
            total = jnp.sum(powers, axis=0, keepdims=True)
            expd[head] = powers
            max_buf[pl.ds(head, 1), :] = row_max
            lse_all[me, pl.ds(head, 1), :] = row_max + jnp.log(jnp.maximum(total, 1e-37))

    def others(m):
        for distance in range(2, line - 1):
            other_round(m, distance)

    def late_rounds(m):
        for distance in range(3, line):
            own_round(m, distance)
        other_round(m, 1)
        side_round(m, line - 1)

    def normalise(first, last):
        @pl.loop(first, last, unroll=2)
        def _(head):
            start = window(head)
            probs = expd[head] * row_buf[pl.ds(head, 1), :]
            expd[head] = probs
            value_grad[:, pl.ds(start, WIN)] += dot_nn(probs.astype(jnp.bfloat16), grad_win[head])

    def fixed(head):
        start = 128 * min((head * HDIM) // 128, (width - WIN) // 128)
        return slice(start, start + WIN)

    def weigh(group_index):
        cols = slice(bounds[group_index], bounds[group_index + 1])
        values[:, cols] = dot_nn(tiles[...], weights[1, :, cols]).astype(jnp.bfloat16)
        for head in members[group_index]:
            part = dot_nt(values[:, fixed(head)], grad_win[head])
            prob_grad[head] = part
            weighted_all[group_index, me, head : head + 1, :] = jnp.sum(
                expd[head] * part, axis=0, keepdims=True
            )
        return spread(
            weighted_all.at[group_index], sum_send.at[group_index], sum_recv.at[group_index]
        )

    def differentiate(group_index):
        collect(weighted_all.at[group_index], sum_send.at[group_index], sum_recv.at[group_index])
        delta = weighted_all[group_index, 0]
        for index in range(1, n_tile):
            delta = delta + weighted_all[group_index, index]
        row_buf[...] = delta
        for head in members[group_index]:
            gap = prob_grad[head] - row_buf[head : head + 1, :]
            dscore = (inv_scale * expd[head] * gap).astype(jnp.bfloat16)
            key_grad[:, fixed(head)] += dot_nn(dscore, query_win[head])

    cuts = [heads * step // 4 for step in range(5)]
    score(cuts[0], cuts[1])
    own_round(1, 1)
    score(cuts[1], cuts[2])
    own_round(1, 2)
    score(cuts[2], cuts[4])
    lse_copies = spread(lse_all, lse_send, lse_recv)
    late_rounds(1)
    open_own(2)
    collect(lse_all, lse_send, lse_recv)
    top = lse_all[0]
    for index in range(1, n_tile):
        top = jnp.maximum(top, lse_all[index])
    total = jnp.exp(lse_all[0] - top)
    for index in range(1, n_tile):
        total = total + jnp.exp(lse_all[index] - top)
    row_buf[...] = jnp.exp(max_buf[...] - (top + jnp.log(total)))

    others(1)
    own_round(2, 1)
    normalise(cuts[0], cuts[2])
    own_round(2, 2)
    normalise(cuts[2], cuts[4])
    sum_copies = []
    for index in range(groups):
        m = index + 1
        close_round(m)
        sum_copies += weigh(index)
        if index + 1 < groups:
            if index > 0:
                own_round(m + 1, 2)
            late_rounds(m + 1)
            if index + 2 < groups:
                open_own(m + 2)
            differentiate(index)
            others(m + 1)
            if index + 2 < groups:
                own_round(m + 2, 1)

    value_cast = value_grad[...].astype(jnp.bfloat16)
    ready = members[-1][0] * HDIM // 128 * 128
    early_cast = key_grad[:, :ready].astype(jnp.bfloat16)

    @pl.loop(0, 2 * chunks, unroll=2)
    def _(index):
        rows = pl.ds(pl.multiple_of(index * WIN, WIN), WIN)
        part = dot_nt(value_cast, weights[1, rows, :])
        acc[index] = part + dot_nt(early_cast, weights[0, rows, :ready])

    differentiate(groups - 1)
    key_cast = key_grad[:, ready:].astype(jnp.bfloat16)

    def pair_copy(index):
        columns = pl.ds(index * WIN, WIN)
        return pltpu.make_async_remote_copy(
            src_ref=to_pair.at[:, columns],
            dst_ref=pair_ref.at[:, columns],
            send_sem=pair_send.at[index],
            recv_sem=pair_recv.at[index],
            device_id={"head": 1 - group},
            device_id_type=MESH,
        )

    def partial_sum(chunk):
        rows = pl.ds(pl.multiple_of(chunk * WIN, WIN), WIN)
        return (acc[chunk] + dot_nt(key_cast, weights[0, rows, ready:])).astype(jnp.bfloat16)

    for index in range(chunks):
        to_pair[:, index * WIN : (index + 1) * WIN] = partial_sum(chunks * (1 - group) + index)
        pair_copy(index).start()
    for index in range(chunks):
        own_ref[:, index * WIN : (index + 1) * WIN] = partial_sum(chunks * group + index)

    for index in range(chunks):
        pair_copy(index).wait_recv()
    for index in range(chunks):
        pair_copy(index).wait_send()
    for copy in lse_copies + sum_copies:
        copy.wait_send()
    assert len(started) <= SENDS
    for index, (cond, what) in enumerate(started):
        if cond is None:
            remote(index, *what).wait_send()
        else:
            pl.when(cond)(functools.partial(lambda i, w: remote(i, *w).wait_send(), index, what))


def fused_device(across, tiles_in, key_weight, value_weight, queries, out_grad, valid_count, tile_mask):
    n_tile = lax.axis_size("tile")
    tile_dev, depth = tiles_in.shape[1:]
    latents, width = queries.shape
    shard = key_weight.shape[0]
    heads = width // HDIM
    chunks = depth // 2 // WIN
    groups = pl.cdiv(width, WIN)
    bf16, f32 = jnp.bfloat16, jnp.float32
    dma = pltpu.SemaphoreType.DMA
    own, pair = pl.pallas_call(
        functools.partial(fused, n_tile // across, across, shard, width, heads, chunks),
        out_shape=[jax.ShapeDtypeStruct((tile_dev, depth // 2), bf16)] * 2,
        in_specs=[pl.BlockSpec(memory_space=pl.ANY)] * 5
        + [pl.BlockSpec(memory_space=pltpu.SMEM), pl.BlockSpec(memory_space=pltpu.VMEM)],
        out_specs=[pl.BlockSpec(memory_space=pltpu.VMEM)] * 2,
        scratch_shapes=[
            pltpu.VMEM((2, depth, width), bf16),
            pltpu.VMEM((tile_dev, depth), bf16),
            pltpu.VMEM((latents, width), bf16),
            pltpu.VMEM((latents, width), bf16),
            pltpu.VMEM((heads, latents, WIN), bf16),
            pltpu.VMEM((heads, latents, WIN), bf16),
            pltpu.VMEM((3, tile_dev, width), bf16),
            pltpu.VMEM((tile_dev, width), bf16),
            pltpu.VMEM((heads, tile_dev, latents), f32),
            pltpu.VMEM((heads, tile_dev, latents), f32),
            pltpu.VMEM((heads, latents), f32),
            pltpu.VMEM((n_tile, heads, latents), f32),
            pltpu.VMEM((groups, n_tile, heads, latents), f32),
            pltpu.VMEM((heads, latents), f32),
            pltpu.VMEM((tile_dev, width), f32),
            pltpu.VMEM((tile_dev, width), f32),
            pltpu.VMEM((2 * chunks, tile_dev, WIN), f32),
            pltpu.VMEM((tile_dev, chunks * WIN), bf16),
            pltpu.VMEM((tile_dev, 128), f32),
            dma((5,)),
            dma((SENDS,)),
            dma((n_tile * 2 * (SUBS + groups),)),
            dma((n_tile,)),
            dma((n_tile,)),
            dma((groups, n_tile)),
            dma((groups, n_tile)),
            dma((chunks,)),
            dma((chunks,)),
        ],
        compiler_params=pltpu.CompilerParams(
            collective_id=0, has_side_effects=True, vmem_limit_bytes=56 * 2**20
        ),
        cost_estimate=pl.CostEstimate(
            flops=4 * tile_dev * depth * width * 2, bytes_accessed=8 * 2**20, transcendentals=2**20
        ),
    )(tiles_in, key_weight, value_weight, queries, out_grad, valid_count, tile_mask)
    return (own.astype(f32) + pair.astype(f32)).astype(bf16)[None]


def solution(mesh):
    across = mesh.shape["dp"]

    def device(tiles_in, key_weight, *rest):
        fits = (
            across == 2
            and mesh.shape["head"] == 2
            and mesh.shape["tile"] >= 3 * across
            and key_weight.shape[0] % (32 * SUBS) == 0
            and tiles_in.shape[2] % (2 * WIN) == 0
        )
        body = functools.partial(fused_device, across) if fits else per_device
        return body(tiles_in, key_weight, *rest)

    return jax.shard_map(
        device,
        mesh=mesh,
        in_specs=(
            P("dp", "tile", None),
            P("tile", "head"),
            P("tile", "head"),
            P(None, "head"),
            P("dp", None, "head"),
            P("dp"),
            P("dp", "tile"),
        ),
        out_specs=P("dp", "tile", "head"),
        check_vma=False,
    )
```

```python
import functools

import jax
import jax.numpy as jnp
from jax import lax
from jax.experimental import pallas as pl
from jax.experimental.pallas import tpu as pltpu
from jax.sharding import PartitionSpec as P

HDIM = 80


NEG_LARGE = -1e30
NEG_FLOOR = -1e29
WIN = 256
SUBS = 2
SENDS = 192
UP, DOWN, ACROSS, TWIN = range(4)
MESH = pl.DeviceIdType.MESH


def per_device(tiles_in, key_weight, value_weight, queries, out_grad, valid_count, tile_mask):
    inv_scale = HDIM ** (-0.5)
    tile_dev = tiles_in.shape[1]
    group_width = queries.shape[1]
    heads_here = group_width // HDIM
    latents = queries.shape[0]
    local_tiles = tiles_in[0]
    positions = lax.axis_index("tile") * tile_dev + jnp.arange(tile_dev, dtype=jnp.int32)
    kept = (tile_mask[0] == 1) | (positions == 0)
    valid = ((positions < valid_count[0]) & kept)[None, None, :]
    full_key, full_value = (
        lax.all_gather(key_weight, "tile", axis=0, tiled=True),
        lax.all_gather(value_weight, "tile", axis=0, tiled=True),
    )
    keys = jnp.dot(local_tiles, full_key, preferred_element_type=jnp.float32)
    values = jnp.dot(local_tiles, full_value, preferred_element_type=jnp.float32).astype(
        jnp.bfloat16
    )
    query_heads = queries.reshape(latents, heads_here, HDIM)
    query_wide = queries.astype(jnp.float32).reshape(latents, heads_here, HDIM)
    key_heads = keys.reshape(tile_dev, heads_here, HDIM)
    value_heads = values.reshape(tile_dev, heads_here, HDIM)
    grad_heads = out_grad[0].reshape(latents, heads_here, HDIM)
    scores = (
        jnp.einsum(
            "lhd,thd->hlt",
            query_wide,
            key_heads,
            precision=lax.Precision.HIGHEST,
            preferred_element_type=jnp.float32,
        )
        * inv_scale
    )
    prob_grad = jnp.einsum(
        "lhd,thd->hlt", grad_heads, value_heads, preferred_element_type=jnp.float32
    )
    local_max = jnp.max(jnp.where(valid, scores, NEG_LARGE), axis=2)
    row_max = lax.pmax(local_max, "tile")
    expd = jnp.where(valid, jnp.exp(scores - row_max[:, :, None]), 0.0)
    total, weighted = lax.psum((jnp.sum(expd, axis=2), jnp.sum(expd * prob_grad, axis=2)), "tile")
    delta = weighted / total
    probs = expd / total[:, :, None]
    dscore = (inv_scale * probs * (prob_grad - delta[:, :, None])).astype(jnp.bfloat16)
    value_grad = (
        jnp.einsum(
            "hlt,lhd->thd",
            probs.astype(jnp.bfloat16),
            grad_heads,
            preferred_element_type=jnp.float32,
        )
        .astype(jnp.bfloat16)
        .reshape(tile_dev, group_width)
    )
    key_grad = (
        jnp.einsum("hlt,lhd->thd", dscore, query_heads, preferred_element_type=jnp.float32)
        .astype(jnp.bfloat16)
        .reshape(tile_dev, group_width)
    )
    partial_sum = jnp.einsum("tc,rc->tr", key_grad, full_key, preferred_element_type=jnp.float32)
    partial_sum = partial_sum + jnp.einsum(
        "tc,rc->tr", value_grad, full_value, preferred_element_type=jnp.float32
    )
    rounded = partial_sum.astype(jnp.bfloat16)
    summed = lax.psum_scatter(rounded[None], "head", scatter_dimension=2, tiled=True).astype(
        jnp.float32
    )
    return summed.astype(jnp.bfloat16)


def dot_nt(a, b):
    return lax.dot_general(a, b, (((1,), (1,)), ((), ())), preferred_element_type=jnp.float32)


def dot_nn(a, b):
    return jnp.dot(a, b, preferred_element_type=jnp.float32)


def fused(
    line, across, shard, width, heads, chunks,
    tiles_hbm, key_hbm, value_hbm, query_hbm, grad_hbm, count_ref, mask_ref,
    own_ref, pair_ref,
    weights, tiles, query, grad, query_win, grad_win, query_turn, grad_turn, key_parts, values, expd, prob_grad,
    max_buf, lse_all, weighted_all, row_buf, value_grad, key_grad, acc, to_pair, valid,
    local_sem, send_sem, recv_sem, lse_send, lse_recv, sum_send, sum_recv, pair_send, pair_recv,
):
    n_tile = line * across
    half = shard // 2
    size = half // SUBS
    inv_scale = HDIM ** (-0.5)
    me = lax.axis_index("tile")
    slide = lax.axis_index("dp")
    group = lax.axis_index("head")
    z = me // across
    x = me % across
    beside = me + 1 - 2 * x
    twin = slide + 1 - 2 * (slide % 2)
    mine, other = slide % 2, 1 - slide % 2
    devices = {
        UP: {"tile": me + across},
        DOWN: {"tile": me - across},
        ACROSS: {"tile": beside},
        TWIN: {"dp": twin},
    }
    sources = (key_hbm, value_hbm)
    started = []

    def copy_in(src, dst, index):
        copy = pltpu.make_async_copy(src, dst, local_sem.at[index])
        copy.start()
        return copy

    own_rows = pl.ds(pl.multiple_of(me * shard, 16), shard)
    query_copy = copy_in(query_hbm, query, 0)
    grad_copy = copy_in(grad_hbm.at[0], grad, 1)
    tiles_copy = copy_in(tiles_hbm.at[0], tiles, 2)
    own_copies = [copy_in(sources[m], weights.at[m, own_rows], 3 + m) for m in range(2)]

    barrier = pltpu.get_barrier_semaphore()
    for step in range(1, n_tile):
        pl.semaphore_signal(
            barrier, inc=1, device_id={"tile": (me + step) % n_tile}, device_id_type=MESH
        )
    pl.semaphore_signal(barrier, inc=1, device_id={"dp": twin}, device_id_type=MESH)
    pl.semaphore_signal(barrier, inc=1, device_id={"head": 1 - group}, device_id_type=MESH)
    pl.semaphore_wait(barrier, n_tile + 1)

    def piece(m, owner, part, sub, way, first=False):
        offset = part * half + sub * size
        rows = pl.ds(pl.multiple_of(owner * shard + offset, 16), size)
        src = weights.at[m, rows]
        if first:
            src = sources[m].at[pl.ds(pl.multiple_of(offset, 16), size)]
        return src, weights.at[m, rows], ((m * n_tile + owner) * 2 + part) * SUBS + sub, devices[way]

    def remote(index, *what):
        src, dst, landing, device = piece(*what)
        return pltpu.make_async_remote_copy(
            src_ref=src,
            dst_ref=dst,
            send_sem=send_sem.at[index],
            recv_sem=recv_sem.at[landing],
            device_id=device,
            device_id_type=MESH,
        )

    def send(cond, *what):
        index = len(started)
        started.append((cond, what))
        if cond is None:
            remote(index, *what).start()
        else:
            pl.when(cond)(lambda: remote(index, *what).start())

    def arrive(cond, m, owner, part, sub):
        if cond is None:
            remote(0, m, owner, part, sub, ACROSS).wait_recv()
        else:
            pl.when(cond)(lambda: remote(0, m, owner, part, sub, ACROSS).wait_recv())

    def both(a, b):
        return b if a is None else (a if b is None else jnp.logical_and(a, b))

    can_up, can_down = z < line - 1, z > 0
    ways = ((UP, can_up), (DOWN, can_down))

    def held_at(base, distance):
        if distance == 0:
            return [(None, base)]
        return [
            (z >= distance, base - distance * across),
            (z + distance < line, base + distance * across),
        ]

    def open_own(m):
        for sub in range(SUBS):
            for way, can in ways:
                send(can, m, me, mine, sub, way, True)

    def open_side(m):
        for sub in range(SUBS):
            send(None, m, me, mine, sub, ACROSS, True)

    def side_round(m, distance):
        for sub in range(SUBS):
            for there, owner in held_at(beside, distance):
                arrive(there, m, owner, mine, sub)
                send(there, m, owner, mine, sub, TWIN)

    def own_round(m, distance):
        last = distance == line - 1
        for sub in range(SUBS):
            for (there, owner), (way, can) in zip(held_at(me, distance), ways):
                arrive(there, m, owner, mine, sub)
                if not last:
                    send(both(there, can), m, owner, mine, sub, way)
                send(there, m, owner, mine, sub, ACROSS)
                if last:
                    send(there, m, owner, mine, sub, TWIN)
        for way, can, ends in ((UP, can_up, z), (DOWN, can_down, line - 1 - z)):
            turn = jnp.maximum(ends, 1) == distance
            for sub in range(SUBS):
                send(both(turn, can), m, me, other, sub, way, True)
        side_round(m, distance - 1)

    def other_round(m, distance):
        for sub in range(SUBS):
            for (there, owner), (way, can) in zip(held_at(me, distance), ways):
                arrive(there, m, owner, other, sub)
                if distance + 1 < line - 1:
                    send(both(there, can), m, owner, other, sub, way)

    def close_round(m):
        for sub in range(SUBS):
            for distance in range(line):
                for there, owner in held_at(beside, distance):
                    arrive(there, m, owner, other, sub)
            for there, owner in held_at(me, line - 1):
                arrive(there, m, owner, other, sub)

    def window(head):
        start = 128 * jnp.minimum((head * HDIM) // 128, (width - WIN) // 128)
        return pl.multiple_of(start, 128)

    def fixed(head):
        start = 128 * min((head * HDIM) // 128, (width - WIN) // 128)
        return slice(start, start + WIN)

    def spread(buffer, send_sems, recv_sems):
        copies = []
        for step in range(1, n_tile):
            copies.append(
                pltpu.make_async_remote_copy(
                    src_ref=buffer.at[me],
                    dst_ref=buffer.at[me],
                    send_sem=send_sems.at[step],
                    recv_sem=recv_sems.at[me],
                    device_id={"tile": (me + step) % n_tile},
                    device_id_type=MESH,
                )
            )
            copies[-1].start()
        return copies

    def collect(buffer, send_sems, recv_sems):
        for step in range(1, n_tile):
            owner = (me + n_tile - step) % n_tile
            pltpu.make_async_remote_copy(
                src_ref=buffer.at[owner],
                dst_ref=buffer.at[owner],
                send_sem=send_sems.at[step],
                recv_sem=recv_sems.at[owner],
                device_id={"tile": owner},
                device_id_type=MESH,
            ).wait_recv()

    open_own(0)
    open_side(0)

    positions = me * tiles.shape[0] + lax.broadcasted_iota(jnp.int32, (128, tiles.shape[0]), 1)
    kept = (mask_ref[...] == 1) | (positions == 0)
    valid[...] = jnp.where(kept & (positions < count_ref[0]), 1.0, 0.0).T

    query_copy.wait()
    grad_copy.wait()

    @pl.loop(0, heads)
    def _(head):
        start = window(head)
        column = start + lax.broadcasted_iota(jnp.int32, (query.shape[0], WIN), 1)
        inside = (column >= head * HDIM) & (column < (head + 1) * HDIM)
        for whole, cut, turn in ((query, query_win, query_turn), (grad, grad_win, grad_turn)):
            part = jnp.where(inside, whole[:, pl.ds(start, WIN)].astype(jnp.float32), 0.0)
            cut[head] = part.astype(jnp.bfloat16)
            turn[head] = part.T.astype(jnp.bfloat16)

    value_grad[...] = jnp.zeros_like(value_grad)
    key_grad[...] = jnp.zeros_like(key_grad)

    for distance in range(1, line):
        own_round(0, distance)
    open_side(1)
    other_round(0, 1)
    open_own(1)
    side_round(0, line - 1)
    for distance in range(2, line - 1):
        other_round(0, distance)
    own_round(1, 1)
    close_round(0)

    tiles_copy.wait()
    for copy in own_copies:
        copy.wait()
    keys = dot_nn(tiles[...], weights[0])
    for index in range(3):
        part = keys.astype(jnp.bfloat16)
        key_parts[index] = part
        keys = keys - part.astype(jnp.float32)

    def score(first, last):
        @pl.loop(first, last, unroll=2)
        def _(head):
            start = window(head)
            cut = query_turn[head]
            scores = dot_nn(key_parts[2, :, pl.ds(start, WIN)], cut)
            scores = scores + dot_nn(key_parts[1, :, pl.ds(start, WIN)], cut)
            scores = scores + dot_nn(key_parts[0, :, pl.ds(start, WIN)], cut)
            scores = jnp.where(valid[:, :1] > 0.0, scores * inv_scale, NEG_LARGE)
            row_max = jnp.maximum(jnp.max(scores, axis=0, keepdims=True), NEG_FLOOR)
            powers = jnp.exp(scores - row_max)
            total = jnp.sum(powers, axis=0, keepdims=True)
            expd[head] = powers
            max_buf[pl.ds(head, 1), :] = row_max
            lse_all[me, pl.ds(head, 1), :] = row_max + jnp.log(jnp.maximum(total, 1e-37))

    cuts = [heads * step // 4 for step in range(5)]
    score(cuts[0], cuts[1])
    own_round(1, 2)
    score(cuts[1], cuts[4])
    lse_copies = spread(lse_all, lse_send, lse_recv)
    for distance in range(3, line):
        own_round(1, distance)
    other_round(1, 1)
    side_round(1, line - 1)
    collect(lse_all, lse_send, lse_recv)
    top = lse_all[0]
    for index in range(1, n_tile):
        top = jnp.maximum(top, lse_all[index])
    total = jnp.exp(lse_all[0] - top)
    for index in range(1, n_tile):
        total = total + jnp.exp(lse_all[index] - top)
    row_buf[...] = jnp.exp(max_buf[...] - (top + jnp.log(total)))

    @pl.loop(0, heads, unroll=2)
    def _(head):
        start = window(head)
        probs = expd[head] * row_buf[pl.ds(head, 1), :]
        expd[head] = probs
        value_grad[:, pl.ds(start, WIN)] += dot_nn(probs.astype(jnp.bfloat16), grad_win[head])

    for distance in range(2, line - 1):
        other_round(1, distance)
    close_round(1)

    values[...] = dot_nn(tiles[...], weights[1]).astype(jnp.bfloat16)

    for head in range(heads):
        part = dot_nn(values[:, fixed(head)], grad_turn[head])
        prob_grad[head] = part
        weighted_all[me, head : head + 1, :] = jnp.sum(expd[head] * part, axis=0, keepdims=True)

    sum_copies = spread(weighted_all, sum_send, sum_recv)

    value_cast = value_grad[...].astype(jnp.bfloat16)

    @pl.loop(0, 2 * chunks, unroll=2)
    def _(index):
        rows = pl.ds(pl.multiple_of(index * WIN, WIN), WIN)
        acc[index] = dot_nt(value_cast, weights[1, rows, :])

    collect(weighted_all, sum_send, sum_recv)
    delta = weighted_all[0]
    for index in range(1, n_tile):
        delta = delta + weighted_all[index]
    row_buf[...] = delta

    for head in range(heads):
        gap = prob_grad[head] - row_buf[head : head + 1, :]
        dscore = (inv_scale * expd[head] * gap).astype(jnp.bfloat16)
        key_grad[:, fixed(head)] += dot_nn(dscore, query_win[head])

    key_cast = key_grad[...].astype(jnp.bfloat16)

    def pair_copy(index):
        columns = pl.ds(index * WIN, WIN)
        return pltpu.make_async_remote_copy(
            src_ref=to_pair.at[:, columns],
            dst_ref=pair_ref.at[:, columns],
            send_sem=pair_send.at[index],
            recv_sem=pair_recv.at[index],
            device_id={"head": 1 - group},
            device_id_type=MESH,
        )

    def partial_sum(chunk):
        rows = pl.ds(pl.multiple_of(chunk * WIN, WIN), WIN)
        return (acc[chunk] + dot_nt(key_cast, weights[0, rows, :])).astype(jnp.bfloat16)

    for index in range(chunks):
        to_pair[:, index * WIN : (index + 1) * WIN] = partial_sum(chunks * (1 - group) + index)
        pair_copy(index).start()
    for index in range(chunks):
        own_ref[:, index * WIN : (index + 1) * WIN] = partial_sum(chunks * group + index)

    for index in range(chunks):
        pair_copy(index).wait_recv()
    for index in range(chunks):
        pair_copy(index).wait_send()
    for copy in lse_copies + sum_copies:
        copy.wait_send()
    assert len(started) <= SENDS
    for index, (cond, what) in enumerate(started):
        if cond is None:
            remote(index, *what).wait_send()
        else:
            pl.when(cond)(functools.partial(lambda i, w: remote(i, *w).wait_send(), index, what))


def fused_device(across, tiles_in, key_weight, value_weight, queries, out_grad, valid_count, tile_mask):
    n_tile = lax.axis_size("tile")
    tile_dev, depth = tiles_in.shape[1:]
    latents, width = queries.shape
    shard = key_weight.shape[0]
    heads = width // HDIM
    chunks = depth // 2 // WIN
    bf16, f32 = jnp.bfloat16, jnp.float32
    dma = pltpu.SemaphoreType.DMA
    own, pair = pl.pallas_call(
        functools.partial(fused, n_tile // across, across, shard, width, heads, chunks),
        out_shape=[jax.ShapeDtypeStruct((tile_dev, depth // 2), bf16)] * 2,
        in_specs=[pl.BlockSpec(memory_space=pl.ANY)] * 5
        + [pl.BlockSpec(memory_space=pltpu.SMEM), pl.BlockSpec(memory_space=pltpu.VMEM)],
        out_specs=[pl.BlockSpec(memory_space=pltpu.VMEM)] * 2,
        scratch_shapes=[
            pltpu.VMEM((2, depth, width), bf16),
            pltpu.VMEM((tile_dev, depth), bf16),
            pltpu.VMEM((latents, width), bf16),
            pltpu.VMEM((latents, width), bf16),
            pltpu.VMEM((heads, latents, WIN), bf16),
            pltpu.VMEM((heads, latents, WIN), bf16),
            pltpu.VMEM((heads, WIN, latents), bf16),
            pltpu.VMEM((heads, WIN, latents), bf16),
            pltpu.VMEM((3, tile_dev, width), bf16),
            pltpu.VMEM((tile_dev, width), bf16),
            pltpu.VMEM((heads, tile_dev, latents), f32),
            pltpu.VMEM((heads, tile_dev, latents), f32),
            pltpu.VMEM((heads, latents), f32),
            pltpu.VMEM((n_tile, heads, latents), f32),
            pltpu.VMEM((n_tile, heads, latents), f32),
            pltpu.VMEM((heads, latents), f32),
            pltpu.VMEM((tile_dev, width), f32),
            pltpu.VMEM((tile_dev, width), f32),
            pltpu.VMEM((2 * chunks, tile_dev, WIN), f32),
            pltpu.VMEM((tile_dev, chunks * WIN), bf16),
            pltpu.VMEM((tile_dev, 128), f32),
            dma((5,)),
            dma((SENDS,)),
            dma((2 * n_tile * 2 * SUBS,)),
            dma((n_tile,)),
            dma((n_tile,)),
            dma((n_tile,)),
            dma((n_tile,)),
            dma((chunks,)),
            dma((chunks,)),
        ],
        compiler_params=pltpu.CompilerParams(
            collective_id=0, has_side_effects=True, vmem_limit_bytes=56 * 2**20
        ),
        cost_estimate=pl.CostEstimate(
            flops=4 * tile_dev * depth * width * 2, bytes_accessed=8 * 2**20, transcendentals=2**20
        ),
    )(tiles_in, key_weight, value_weight, queries, out_grad, valid_count, tile_mask)
    return (own.astype(f32) + pair.astype(f32)).astype(bf16)[None]


def solution(mesh):
    across = mesh.shape["dp"]

    def device(tiles_in, key_weight, *rest):
        fits = (
            across == 2
            and mesh.shape["head"] == 2
            and mesh.shape["tile"] >= 3 * across
            and key_weight.shape[0] % (32 * SUBS) == 0
            and tiles_in.shape[2] % (2 * WIN) == 0
        )
        body = functools.partial(fused_device, across) if fits else per_device
        return body(tiles_in, key_weight, *rest)

    return jax.shard_map(
        device,
        mesh=mesh,
        in_specs=(
            P("dp", "tile", None),
            P("tile", "head"),
            P("tile", "head"),
            P(None, "head"),
            P("dp", None, "head"),
            P("dp"),
            P("dp", "tile"),
        ),
        out_specs=P("dp", "tile", "head"),
        check_vma=False,
    )
```

```python
import functools

import jax
import jax.numpy as jnp
from jax import lax
from jax.experimental import pallas as pl
from jax.experimental.pallas import tpu as pltpu
from jax.sharding import PartitionSpec as P

HDIM = 80


NEG_LARGE = -1e30
NEG_FLOOR = -1e29
WIN = 256
SUBS = 2
SENDS = 192
UP, DOWN, ACROSS, TWIN = range(4)
MESH = pl.DeviceIdType.MESH


def per_device(tiles_in, key_weight, value_weight, queries, out_grad, valid_count, tile_mask):
    inv_scale = HDIM ** (-0.5)
    tile_dev = tiles_in.shape[1]
    group_width = queries.shape[1]
    heads_here = group_width // HDIM
    latents = queries.shape[0]
    local_tiles = tiles_in[0]
    positions = lax.axis_index("tile") * tile_dev + jnp.arange(tile_dev, dtype=jnp.int32)
    kept = (tile_mask[0] == 1) | (positions == 0)
    valid = ((positions < valid_count[0]) & kept)[None, None, :]
    full_key, full_value = (
        lax.all_gather(key_weight, "tile", axis=0, tiled=True),
        lax.all_gather(value_weight, "tile", axis=0, tiled=True),
    )
    keys = jnp.dot(local_tiles, full_key, preferred_element_type=jnp.float32)
    values = jnp.dot(local_tiles, full_value, preferred_element_type=jnp.float32).astype(
        jnp.bfloat16
    )
    query_heads = queries.reshape(latents, heads_here, HDIM)
    query_wide = queries.astype(jnp.float32).reshape(latents, heads_here, HDIM)
    key_heads = keys.reshape(tile_dev, heads_here, HDIM)
    value_heads = values.reshape(tile_dev, heads_here, HDIM)
    grad_heads = out_grad[0].reshape(latents, heads_here, HDIM)
    scores = (
        jnp.einsum(
            "lhd,thd->hlt",
            query_wide,
            key_heads,
            precision=lax.Precision.HIGHEST,
            preferred_element_type=jnp.float32,
        )
        * inv_scale
    )
    prob_grad = jnp.einsum(
        "lhd,thd->hlt", grad_heads, value_heads, preferred_element_type=jnp.float32
    )
    local_max = jnp.max(jnp.where(valid, scores, NEG_LARGE), axis=2)
    row_max = lax.pmax(local_max, "tile")
    expd = jnp.where(valid, jnp.exp(scores - row_max[:, :, None]), 0.0)
    total, weighted = lax.psum((jnp.sum(expd, axis=2), jnp.sum(expd * prob_grad, axis=2)), "tile")
    delta = weighted / total
    probs = expd / total[:, :, None]
    dscore = (inv_scale * probs * (prob_grad - delta[:, :, None])).astype(jnp.bfloat16)
    value_grad = (
        jnp.einsum(
            "hlt,lhd->thd",
            probs.astype(jnp.bfloat16),
            grad_heads,
            preferred_element_type=jnp.float32,
        )
        .astype(jnp.bfloat16)
        .reshape(tile_dev, group_width)
    )
    key_grad = (
        jnp.einsum("hlt,lhd->thd", dscore, query_heads, preferred_element_type=jnp.float32)
        .astype(jnp.bfloat16)
        .reshape(tile_dev, group_width)
    )
    partial_sum = jnp.einsum("tc,rc->tr", key_grad, full_key, preferred_element_type=jnp.float32)
    partial_sum = partial_sum + jnp.einsum(
        "tc,rc->tr", value_grad, full_value, preferred_element_type=jnp.float32
    )
    rounded = partial_sum.astype(jnp.bfloat16)
    summed = lax.psum_scatter(rounded[None], "head", scatter_dimension=2, tiled=True).astype(
        jnp.float32
    )
    return summed.astype(jnp.bfloat16)


def dot_nt(a, b):
    return lax.dot_general(a, b, (((1,), (1,)), ((), ())), preferred_element_type=jnp.float32)


def dot_nn(a, b):
    return jnp.dot(a, b, preferred_element_type=jnp.float32)


def fused(
    line, across, shard, width, heads, chunks,
    tiles_hbm, key_hbm, value_hbm, query_hbm, grad_hbm, count_ref, mask_ref,
    own_ref, pair_ref,
    weights, tiles, query, grad, query_win, grad_win, query_turn, grad_turn, key_parts, values, expd, prob_grad,
    max_buf, lse_all, weighted_all, row_buf, value_grad, key_grad, acc, to_pair, valid,
    local_sem, send_sem, recv_sem, lse_send, lse_recv, sum_send, sum_recv, pair_send, pair_recv,
):
    n_tile = line * across
    half = shard // 2
    size = half // SUBS
    inv_scale = HDIM ** (-0.5)
    me = lax.axis_index("tile")
    slide = lax.axis_index("dp")
    group = lax.axis_index("head")
    z = me // across
    x = me % across
    beside = me + 1 - 2 * x
    twin = slide + 1 - 2 * (slide % 2)
    mine, other = slide % 2, 1 - slide % 2
    devices = {
        UP: {"tile": me + across},
        DOWN: {"tile": me - across},
        ACROSS: {"tile": beside},
        TWIN: {"dp": twin},
    }
    sources = (key_hbm, value_hbm)
    started = []

    def copy_in(src, dst, index):
        copy = pltpu.make_async_copy(src, dst, local_sem.at[index])
        copy.start()
        return copy

    own_rows = pl.ds(pl.multiple_of(me * shard, 16), shard)
    query_copy = copy_in(query_hbm, query, 0)
    grad_copy = copy_in(grad_hbm.at[0], grad, 1)
    tiles_copy = copy_in(tiles_hbm.at[0], tiles, 2)
    own_copies = [copy_in(sources[m], weights.at[m, own_rows], 3 + m) for m in range(2)]

    barrier = pltpu.get_barrier_semaphore()
    for step in range(1, n_tile):
        pl.semaphore_signal(
            barrier, inc=1, device_id={"tile": (me + step) % n_tile}, device_id_type=MESH
        )
    pl.semaphore_signal(barrier, inc=1, device_id={"dp": twin}, device_id_type=MESH)
    pl.semaphore_signal(barrier, inc=1, device_id={"head": 1 - group}, device_id_type=MESH)
    pl.semaphore_wait(barrier, n_tile + 1)

    def piece(m, owner, part, sub, way, first=False):
        offset = part * half + sub * size
        rows = pl.ds(pl.multiple_of(owner * shard + offset, 16), size)
        src = weights.at[m, rows]
        if first:
            src = sources[m].at[pl.ds(pl.multiple_of(offset, 16), size)]
        return src, weights.at[m, rows], ((m * n_tile + owner) * 2 + part) * SUBS + sub, devices[way]

    def remote(index, *what):
        src, dst, landing, device = piece(*what)
        return pltpu.make_async_remote_copy(
            src_ref=src,
            dst_ref=dst,
            send_sem=send_sem.at[index],
            recv_sem=recv_sem.at[landing],
            device_id=device,
            device_id_type=MESH,
        )

    def send(cond, *what):
        index = len(started)
        started.append((cond, what))
        if cond is None:
            remote(index, *what).start()
        else:
            pl.when(cond)(lambda: remote(index, *what).start())

    def arrive(cond, m, owner, part, sub):
        if cond is None:
            remote(0, m, owner, part, sub, ACROSS).wait_recv()
        else:
            pl.when(cond)(lambda: remote(0, m, owner, part, sub, ACROSS).wait_recv())

    def both(a, b):
        return b if a is None else (a if b is None else jnp.logical_and(a, b))

    can_up, can_down = z < line - 1, z > 0
    ways = ((UP, can_up), (DOWN, can_down))

    def held_at(base, distance):
        if distance == 0:
            return [(None, base)]
        return [
            (z >= distance, base - distance * across),
            (z + distance < line, base + distance * across),
        ]

    def open_own(m):
        for sub in range(SUBS):
            for way, can in ways:
                send(can, m, me, mine, sub, way, True)

    def open_side(m):
        for sub in range(SUBS):
            send(None, m, me, mine, sub, ACROSS, True)

    def side_round(m, distance):
        for sub in range(SUBS):
            for there, owner in held_at(beside, distance):
                arrive(there, m, owner, mine, sub)
                if distance > 0:
                    send(there, m, owner, mine, sub, TWIN)

    def own_round(m, distance):
        last = distance == line - 1
        for sub in range(SUBS):
            for (there, owner), (way, can) in zip(held_at(me, distance), ways):
                arrive(there, m, owner, mine, sub)
                if not last:
                    send(both(there, can), m, owner, mine, sub, way)
                send(there, m, owner, mine, sub, ACROSS)
                if last:
                    send(there, m, owner, mine, sub, TWIN)
        if last:
            for sub in range(SUBS):
                send(None, m, me, other, sub, ACROSS, True)
        for way, can, ends in ((UP, can_up, z), (DOWN, can_down, line - 1 - z)):
            turn = jnp.maximum(ends, 1) == distance
            for sub in range(SUBS):
                send(both(turn, can), m, me, other, sub, way, True)
        side_round(m, distance - 1)

    def other_round(m, distance):
        for sub in range(SUBS):
            for (there, owner), (way, can) in zip(held_at(me, distance), ways):
                arrive(there, m, owner, other, sub)
                if distance + 1 < line - 1:
                    send(both(there, can), m, owner, other, sub, way)

    def close_round(m):
        for sub in range(SUBS):
            for distance in range(line):
                for there, owner in held_at(beside, distance):
                    arrive(there, m, owner, other, sub)
            for there, owner in held_at(me, line - 1):
                arrive(there, m, owner, other, sub)

    def window(head):
        start = 128 * jnp.minimum((head * HDIM) // 128, (width - WIN) // 128)
        return pl.multiple_of(start, 128)

    def fixed(head):
        start = 128 * min((head * HDIM) // 128, (width - WIN) // 128)
        return slice(start, start + WIN)

    def spread(buffer, send_sems, recv_sems):
        copies = []
        for step in range(1, n_tile):
            copies.append(
                pltpu.make_async_remote_copy(
                    src_ref=buffer.at[me],
                    dst_ref=buffer.at[me],
                    send_sem=send_sems.at[step],
                    recv_sem=recv_sems.at[me],
                    device_id={"tile": (me + step) % n_tile},
                    device_id_type=MESH,
                )
            )
            copies[-1].start()
        return copies

    def collect(buffer, send_sems, recv_sems):
        for step in range(1, n_tile):
            owner = (me + n_tile - step) % n_tile
            pltpu.make_async_remote_copy(
                src_ref=buffer.at[owner],
                dst_ref=buffer.at[owner],
                send_sem=send_sems.at[step],
                recv_sem=recv_sems.at[owner],
                device_id={"tile": owner},
                device_id_type=MESH,
            ).wait_recv()

    open_own(0)
    open_side(0)

    positions = me * tiles.shape[0] + lax.broadcasted_iota(jnp.int32, (128, tiles.shape[0]), 1)
    kept = (mask_ref[...] == 1) | (positions == 0)
    valid[...] = jnp.where(kept & (positions < count_ref[0]), 1.0, 0.0).T

    query_copy.wait()
    grad_copy.wait()

    @pl.loop(0, heads)
    def _(head):
        start = window(head)
        column = start + lax.broadcasted_iota(jnp.int32, (query.shape[0], WIN), 1)
        inside = (column >= head * HDIM) & (column < (head + 1) * HDIM)
        for whole, cut, turn in ((query, query_win, query_turn), (grad, grad_win, grad_turn)):
            part = jnp.where(inside, whole[:, pl.ds(start, WIN)].astype(jnp.float32), 0.0)
            cut[head] = part.astype(jnp.bfloat16)
            turn[head] = part.T.astype(jnp.bfloat16)

    value_grad[...] = jnp.zeros_like(value_grad)
    key_grad[...] = jnp.zeros_like(key_grad)

    for distance in range(1, line):
        own_round(0, distance)
    open_side(1)
    other_round(0, 1)
    open_own(1)
    side_round(0, line - 1)
    for distance in range(2, line - 1):
        other_round(0, distance)
    own_round(1, 1)
    close_round(0)

    tiles_copy.wait()
    for copy in own_copies:
        copy.wait()
    keys = dot_nn(tiles[...], weights[0])
    for index in range(3):
        part = keys.astype(jnp.bfloat16)
        key_parts[index] = part
        keys = keys - part.astype(jnp.float32)

    def score(first, last):
        @pl.loop(first, last, unroll=2)
        def _(head):
            start = window(head)
            cut = query_turn[head]
            scores = dot_nn(key_parts[2, :, pl.ds(start, WIN)], cut)
            scores = scores + dot_nn(key_parts[1, :, pl.ds(start, WIN)], cut)
            scores = scores + dot_nn(key_parts[0, :, pl.ds(start, WIN)], cut)
            scores = jnp.where(valid[:, :1] > 0.0, scores * inv_scale, NEG_LARGE)
            row_max = jnp.maximum(jnp.max(scores, axis=0, keepdims=True), NEG_FLOOR)
            powers = jnp.exp(scores - row_max)
            total = jnp.sum(powers, axis=0, keepdims=True)
            expd[head] = powers
            max_buf[pl.ds(head, 1), :] = row_max
            lse_all[me, pl.ds(head, 1), :] = row_max + jnp.log(jnp.maximum(total, 1e-37))

    cuts = [heads * step // 4 for step in range(5)]
    score(cuts[0], cuts[1])
    own_round(1, 2)
    score(cuts[1], cuts[4])
    lse_copies = spread(lse_all, lse_send, lse_recv)
    for distance in range(3, line):
        own_round(1, distance)
    other_round(1, 1)
    side_round(1, line - 1)
    collect(lse_all, lse_send, lse_recv)
    top = lse_all[0]
    for index in range(1, n_tile):
        top = jnp.maximum(top, lse_all[index])
    total = jnp.exp(lse_all[0] - top)
    for index in range(1, n_tile):
        total = total + jnp.exp(lse_all[index] - top)
    row_buf[...] = jnp.exp(max_buf[...] - (top + jnp.log(total)))

    @pl.loop(0, heads, unroll=2)
    def _(head):
        start = window(head)
        probs = expd[head] * row_buf[pl.ds(head, 1), :]
        expd[head] = probs
        value_grad[:, pl.ds(start, WIN)] += dot_nn(probs.astype(jnp.bfloat16), grad_win[head])

    for distance in range(2, line - 1):
        other_round(1, distance)
    close_round(1)

    values[...] = dot_nn(tiles[...], weights[1]).astype(jnp.bfloat16)

    for head in range(heads):
        part = dot_nn(values[:, fixed(head)], grad_turn[head])
        prob_grad[head] = part
        weighted_all[me, head : head + 1, :] = jnp.sum(expd[head] * part, axis=0, keepdims=True)

    sum_copies = spread(weighted_all, sum_send, sum_recv)

    value_cast = value_grad[...].astype(jnp.bfloat16)

    @pl.loop(0, 2 * chunks, unroll=2)
    def _(index):
        rows = pl.ds(pl.multiple_of(index * WIN, WIN), WIN)
        acc[index] = dot_nt(value_cast, weights[1, rows, :])

    collect(weighted_all, sum_send, sum_recv)
    delta = weighted_all[0]
    for index in range(1, n_tile):
        delta = delta + weighted_all[index]
    row_buf[...] = delta

    for head in range(heads):
        gap = prob_grad[head] - row_buf[head : head + 1, :]
        dscore = (inv_scale * expd[head] * gap).astype(jnp.bfloat16)
        key_grad[:, fixed(head)] += dot_nn(dscore, query_win[head])

    key_cast = key_grad[...].astype(jnp.bfloat16)

    def pair_copy(index):
        columns = pl.ds(index * WIN, WIN)
        return pltpu.make_async_remote_copy(
            src_ref=to_pair.at[:, columns],
            dst_ref=pair_ref.at[:, columns],
            send_sem=pair_send.at[index],
            recv_sem=pair_recv.at[index],
            device_id={"head": 1 - group},
            device_id_type=MESH,
        )

    def partial_sum(chunk):
        rows = pl.ds(pl.multiple_of(chunk * WIN, WIN), WIN)
        return (acc[chunk] + dot_nt(key_cast, weights[0, rows, :])).astype(jnp.bfloat16)

    for index in range(chunks):
        to_pair[:, index * WIN : (index + 1) * WIN] = partial_sum(chunks * (1 - group) + index)
        pair_copy(index).start()
    for index in range(chunks):
        own_ref[:, index * WIN : (index + 1) * WIN] = partial_sum(chunks * group + index)

    for index in range(chunks):
        pair_copy(index).wait_recv()
    for index in range(chunks):
        pair_copy(index).wait_send()
    for copy in lse_copies + sum_copies:
        copy.wait_send()
    assert len(started) <= SENDS
    for index, (cond, what) in enumerate(started):
        if cond is None:
            remote(index, *what).wait_send()
        else:
            pl.when(cond)(functools.partial(lambda i, w: remote(i, *w).wait_send(), index, what))


def fused_device(across, tiles_in, key_weight, value_weight, queries, out_grad, valid_count, tile_mask):
    n_tile = lax.axis_size("tile")
    tile_dev, depth = tiles_in.shape[1:]
    latents, width = queries.shape
    shard = key_weight.shape[0]
    heads = width // HDIM
    chunks = depth // 2 // WIN
    bf16, f32 = jnp.bfloat16, jnp.float32
    dma = pltpu.SemaphoreType.DMA
    own, pair = pl.pallas_call(
        functools.partial(fused, n_tile // across, across, shard, width, heads, chunks),
        out_shape=[jax.ShapeDtypeStruct((tile_dev, depth // 2), bf16)] * 2,
        in_specs=[pl.BlockSpec(memory_space=pl.ANY)] * 5
        + [pl.BlockSpec(memory_space=pltpu.SMEM), pl.BlockSpec(memory_space=pltpu.VMEM)],
        out_specs=[pl.BlockSpec(memory_space=pltpu.VMEM)] * 2,
        scratch_shapes=[
            pltpu.VMEM((2, depth, width), bf16),
            pltpu.VMEM((tile_dev, depth), bf16),
            pltpu.VMEM((latents, width), bf16),
            pltpu.VMEM((latents, width), bf16),
            pltpu.VMEM((heads, latents, WIN), bf16),
            pltpu.VMEM((heads, latents, WIN), bf16),
            pltpu.VMEM((heads, WIN, latents), bf16),
            pltpu.VMEM((heads, WIN, latents), bf16),
            pltpu.VMEM((3, tile_dev, width), bf16),
            pltpu.VMEM((tile_dev, width), bf16),
            pltpu.VMEM((heads, tile_dev, latents), f32),
            pltpu.VMEM((heads, tile_dev, latents), f32),
            pltpu.VMEM((heads, latents), f32),
            pltpu.VMEM((n_tile, heads, latents), f32),
            pltpu.VMEM((n_tile, heads, latents), f32),
            pltpu.VMEM((heads, latents), f32),
            pltpu.VMEM((tile_dev, width), f32),
            pltpu.VMEM((tile_dev, width), f32),
            pltpu.VMEM((2 * chunks, tile_dev, WIN), f32),
            pltpu.VMEM((tile_dev, chunks * WIN), bf16),
            pltpu.VMEM((tile_dev, 128), f32),
            dma((5,)),
            dma((SENDS,)),
            dma((2 * n_tile * 2 * SUBS,)),
            dma((n_tile,)),
            dma((n_tile,)),
            dma((n_tile,)),
            dma((n_tile,)),
            dma((chunks,)),
            dma((chunks,)),
        ],
        compiler_params=pltpu.CompilerParams(
            collective_id=0, has_side_effects=True, vmem_limit_bytes=56 * 2**20
        ),
        cost_estimate=pl.CostEstimate(
            flops=4 * tile_dev * depth * width * 2, bytes_accessed=8 * 2**20, transcendentals=2**20
        ),
    )(tiles_in, key_weight, value_weight, queries, out_grad, valid_count, tile_mask)
    return (own.astype(f32) + pair.astype(f32)).astype(bf16)[None]


def solution(mesh):
    across = mesh.shape["dp"]

    def device(tiles_in, key_weight, *rest):
        fits = (
            across == 2
            and mesh.shape["head"] == 2
            and mesh.shape["tile"] >= 3 * across
            and key_weight.shape[0] % (32 * SUBS) == 0
            and tiles_in.shape[2] % (2 * WIN) == 0
        )
        body = functools.partial(fused_device, across) if fits else per_device
        return body(tiles_in, key_weight, *rest)

    return jax.shard_map(
        device,
        mesh=mesh,
        in_specs=(
            P("dp", "tile", None),
            P("tile", "head"),
            P("tile", "head"),
            P(None, "head"),
            P("dp", None, "head"),
            P("dp"),
            P("dp", "tile"),
        ),
        out_specs=P("dp", "tile", "head"),
        check_vma=False,
    )
```

```python
import functools

import jax
import jax.numpy as jnp
from jax import lax
from jax.experimental import pallas as pl
from jax.experimental.pallas import tpu as pltpu
from jax.sharding import PartitionSpec as P

HDIM = 80


NEG_LARGE = -1e30
NEG_FLOOR = -1e29
WIN = 256
SUBS = 1
SENDS = 192
UP, DOWN, ACROSS, TWIN = range(4)
MESH = pl.DeviceIdType.MESH


def per_device(tiles_in, key_weight, value_weight, queries, out_grad, valid_count, tile_mask):
    inv_scale = HDIM ** (-0.5)
    tile_dev = tiles_in.shape[1]
    group_width = queries.shape[1]
    heads_here = group_width // HDIM
    latents = queries.shape[0]
    local_tiles = tiles_in[0]
    positions = lax.axis_index("tile") * tile_dev + jnp.arange(tile_dev, dtype=jnp.int32)
    kept = (tile_mask[0] == 1) | (positions == 0)
    valid = ((positions < valid_count[0]) & kept)[None, None, :]
    full_key, full_value = (
        lax.all_gather(key_weight, "tile", axis=0, tiled=True),
        lax.all_gather(value_weight, "tile", axis=0, tiled=True),
    )
    keys = jnp.dot(local_tiles, full_key, preferred_element_type=jnp.float32)
    values = jnp.dot(local_tiles, full_value, preferred_element_type=jnp.float32).astype(
        jnp.bfloat16
    )
    query_heads = queries.reshape(latents, heads_here, HDIM)
    query_wide = queries.astype(jnp.float32).reshape(latents, heads_here, HDIM)
    key_heads = keys.reshape(tile_dev, heads_here, HDIM)
    value_heads = values.reshape(tile_dev, heads_here, HDIM)
    grad_heads = out_grad[0].reshape(latents, heads_here, HDIM)
    scores = (
        jnp.einsum(
            "lhd,thd->hlt",
            query_wide,
            key_heads,
            precision=lax.Precision.HIGHEST,
            preferred_element_type=jnp.float32,
        )
        * inv_scale
    )
    prob_grad = jnp.einsum(
        "lhd,thd->hlt", grad_heads, value_heads, preferred_element_type=jnp.float32
    )
    local_max = jnp.max(jnp.where(valid, scores, NEG_LARGE), axis=2)
    row_max = lax.pmax(local_max, "tile")
    expd = jnp.where(valid, jnp.exp(scores - row_max[:, :, None]), 0.0)
    total, weighted = lax.psum((jnp.sum(expd, axis=2), jnp.sum(expd * prob_grad, axis=2)), "tile")
    delta = weighted / total
    probs = expd / total[:, :, None]
    dscore = (inv_scale * probs * (prob_grad - delta[:, :, None])).astype(jnp.bfloat16)
    value_grad = (
        jnp.einsum(
            "hlt,lhd->thd",
            probs.astype(jnp.bfloat16),
            grad_heads,
            preferred_element_type=jnp.float32,
        )
        .astype(jnp.bfloat16)
        .reshape(tile_dev, group_width)
    )
    key_grad = (
        jnp.einsum("hlt,lhd->thd", dscore, query_heads, preferred_element_type=jnp.float32)
        .astype(jnp.bfloat16)
        .reshape(tile_dev, group_width)
    )
    partial_sum = jnp.einsum("tc,rc->tr", key_grad, full_key, preferred_element_type=jnp.float32)
    partial_sum = partial_sum + jnp.einsum(
        "tc,rc->tr", value_grad, full_value, preferred_element_type=jnp.float32
    )
    rounded = partial_sum.astype(jnp.bfloat16)
    summed = lax.psum_scatter(rounded[None], "head", scatter_dimension=2, tiled=True).astype(
        jnp.float32
    )
    return summed.astype(jnp.bfloat16)


def dot_nt(a, b):
    return lax.dot_general(a, b, (((1,), (1,)), ((), ())), preferred_element_type=jnp.float32)


def dot_nn(a, b):
    return jnp.dot(a, b, preferred_element_type=jnp.float32)


def fused(
    line, across, shard, width, heads, chunks,
    tiles_hbm, key_hbm, value_hbm, query_hbm, grad_hbm, count_ref, mask_ref,
    own_ref, pair_ref,
    weights, tiles, query, grad, query_win, grad_win, query_turn, grad_turn, key_parts, values, expd, prob_grad,
    max_buf, lse_all, weighted_all, row_buf, value_grad, key_grad, acc, to_pair, valid,
    local_sem, send_sem, recv_sem, lse_send, lse_recv, sum_send, sum_recv, pair_send, pair_recv,
):
    n_tile = line * across
    half = shard // 2
    size = half // SUBS
    inv_scale = HDIM ** (-0.5)
    me = lax.axis_index("tile")
    slide = lax.axis_index("dp")
    group = lax.axis_index("head")
    z = me // across
    x = me % across
    beside = me + 1 - 2 * x
    twin = slide + 1 - 2 * (slide % 2)
    mine, other = slide % 2, 1 - slide % 2
    devices = {
        UP: {"tile": me + across},
        DOWN: {"tile": me - across},
        ACROSS: {"tile": beside},
        TWIN: {"dp": twin},
    }
    sources = (key_hbm, value_hbm)
    started = []

    def copy_in(src, dst, index):
        copy = pltpu.make_async_copy(src, dst, local_sem.at[index])
        copy.start()
        return copy

    own_rows = pl.ds(pl.multiple_of(me * shard, 16), shard)
    query_copy = copy_in(query_hbm, query, 0)
    grad_copy = copy_in(grad_hbm.at[0], grad, 1)
    tiles_copy = copy_in(tiles_hbm.at[0], tiles, 2)
    own_copies = [copy_in(sources[m], weights.at[m, own_rows], 3 + m) for m in range(2)]

    barrier = pltpu.get_barrier_semaphore()
    for step in range(1, n_tile):
        pl.semaphore_signal(
            barrier, inc=1, device_id={"tile": (me + step) % n_tile}, device_id_type=MESH
        )
    pl.semaphore_signal(barrier, inc=1, device_id={"dp": twin}, device_id_type=MESH)
    pl.semaphore_signal(barrier, inc=1, device_id={"head": 1 - group}, device_id_type=MESH)
    pl.semaphore_wait(barrier, n_tile + 1)

    def piece(m, owner, part, sub, way, first=False):
        offset = part * half + sub * size
        rows = pl.ds(pl.multiple_of(owner * shard + offset, 16), size)
        src = weights.at[m, rows]
        if first:
            src = sources[m].at[pl.ds(pl.multiple_of(offset, 16), size)]
        return src, weights.at[m, rows], ((m * n_tile + owner) * 2 + part) * SUBS + sub, devices[way]

    def remote(index, *what):
        src, dst, landing, device = piece(*what)
        return pltpu.make_async_remote_copy(
            src_ref=src,
            dst_ref=dst,
            send_sem=send_sem.at[index],
            recv_sem=recv_sem.at[landing],
            device_id=device,
            device_id_type=MESH,
        )

    def send(cond, *what):
        index = len(started)
        started.append((cond, what))
        if cond is None:
            remote(index, *what).start()
        else:
            pl.when(cond)(lambda: remote(index, *what).start())

    def arrive(cond, m, owner, part, sub):
        if cond is None:
            remote(0, m, owner, part, sub, ACROSS).wait_recv()
        else:
            pl.when(cond)(lambda: remote(0, m, owner, part, sub, ACROSS).wait_recv())

    def both(a, b):
        return b if a is None else (a if b is None else jnp.logical_and(a, b))

    can_up, can_down = z < line - 1, z > 0
    ways = ((UP, can_up), (DOWN, can_down))

    def held_at(base, distance):
        if distance == 0:
            return [(None, base)]
        return [
            (z >= distance, base - distance * across),
            (z + distance < line, base + distance * across),
        ]

    def open_own(m):
        for sub in range(SUBS):
            for way, can in ways:
                send(can, m, me, mine, sub, way, True)

    def open_side(m):
        for sub in range(SUBS):
            send(None, m, me, mine, sub, ACROSS, True)

    def side_round(m, distance):
        for sub in range(SUBS):
            for there, owner in held_at(beside, distance):
                arrive(there, m, owner, mine, sub)
                if distance > 0:
                    send(there, m, owner, mine, sub, TWIN)

    def own_round(m, distance):
        last = distance == line - 1
        for sub in range(SUBS):
            for (there, owner), (way, can) in zip(held_at(me, distance), ways):
                arrive(there, m, owner, mine, sub)
                if not last:
                    send(both(there, can), m, owner, mine, sub, way)
                send(there, m, owner, mine, sub, ACROSS)
                if last:
                    send(there, m, owner, mine, sub, TWIN)
        if last:
            for sub in range(SUBS):
                send(None, m, me, other, sub, ACROSS, True)
        for way, can, ends in ((UP, can_up, z), (DOWN, can_down, line - 1 - z)):
            turn = jnp.maximum(ends, 1) == distance
            for sub in range(SUBS):
                send(both(turn, can), m, me, other, sub, way, True)
        side_round(m, distance - 1)

    def other_round(m, distance):
        for sub in range(SUBS):
            for (there, owner), (way, can) in zip(held_at(me, distance), ways):
                arrive(there, m, owner, other, sub)
                if distance + 1 < line - 1:
                    send(both(there, can), m, owner, other, sub, way)

    def close_round(m):
        for sub in range(SUBS):
            for distance in range(line):
                for there, owner in held_at(beside, distance):
                    arrive(there, m, owner, other, sub)
            for there, owner in held_at(me, line - 1):
                arrive(there, m, owner, other, sub)

    def window(head):
        start = 128 * jnp.minimum((head * HDIM) // 128, (width - WIN) // 128)
        return pl.multiple_of(start, 128)

    def fixed(head):
        start = 128 * min((head * HDIM) // 128, (width - WIN) // 128)
        return slice(start, start + WIN)

    def spread(buffer, send_sems, recv_sems):
        copies = []
        for step in range(1, n_tile):
            copies.append(
                pltpu.make_async_remote_copy(
                    src_ref=buffer.at[me],
                    dst_ref=buffer.at[me],
                    send_sem=send_sems.at[step],
                    recv_sem=recv_sems.at[me],
                    device_id={"tile": (me + step) % n_tile},
                    device_id_type=MESH,
                )
            )
            copies[-1].start()
        return copies

    def collect(buffer, send_sems, recv_sems):
        for step in range(1, n_tile):
            owner = (me + n_tile - step) % n_tile
            pltpu.make_async_remote_copy(
                src_ref=buffer.at[owner],
                dst_ref=buffer.at[owner],
                send_sem=send_sems.at[step],
                recv_sem=recv_sems.at[owner],
                device_id={"tile": owner},
                device_id_type=MESH,
            ).wait_recv()

    open_own(0)
    open_side(0)

    positions = me * tiles.shape[0] + lax.broadcasted_iota(jnp.int32, (128, tiles.shape[0]), 1)
    kept = (mask_ref[...] == 1) | (positions == 0)
    valid[...] = jnp.where(kept & (positions < count_ref[0]), 1.0, 0.0).T

    query_copy.wait()
    grad_copy.wait()

    @pl.loop(0, heads)
    def _(head):
        start = window(head)
        column = start + lax.broadcasted_iota(jnp.int32, (query.shape[0], WIN), 1)
        inside = (column >= head * HDIM) & (column < (head + 1) * HDIM)
        for whole, cut, turn in ((query, query_win, query_turn), (grad, grad_win, grad_turn)):
            part = jnp.where(inside, whole[:, pl.ds(start, WIN)].astype(jnp.float32), 0.0)
            cut[head] = part.astype(jnp.bfloat16)
            turn[head] = part.T.astype(jnp.bfloat16)

    value_grad[...] = jnp.zeros_like(value_grad)
    key_grad[...] = jnp.zeros_like(key_grad)

    for distance in range(1, line):
        own_round(0, distance)
    open_side(1)
    other_round(0, 1)
    open_own(1)
    side_round(0, line - 1)
    for distance in range(2, line - 1):
        other_round(0, distance)
    own_round(1, 1)
    close_round(0)

    tiles_copy.wait()
    for copy in own_copies:
        copy.wait()
    keys = dot_nn(tiles[...], weights[0])
    for index in range(3):
        part = keys.astype(jnp.bfloat16)
        key_parts[index] = part
        keys = keys - part.astype(jnp.float32)

    def score(first, last):
        @pl.loop(first, last, unroll=2)
        def _(head):
            start = window(head)
            cut = query_turn[head]
            scores = dot_nn(key_parts[2, :, pl.ds(start, WIN)], cut)
            scores = scores + dot_nn(key_parts[1, :, pl.ds(start, WIN)], cut)
            scores = scores + dot_nn(key_parts[0, :, pl.ds(start, WIN)], cut)
            scores = jnp.where(valid[:, :1] > 0.0, scores * inv_scale, NEG_LARGE)
            row_max = jnp.maximum(jnp.max(scores, axis=0, keepdims=True), NEG_FLOOR)
            powers = jnp.exp(scores - row_max)
            total = jnp.sum(powers, axis=0, keepdims=True)
            expd[head] = powers
            max_buf[pl.ds(head, 1), :] = row_max
            lse_all[me, pl.ds(head, 1), :] = row_max + jnp.log(jnp.maximum(total, 1e-37))

    cuts = [heads * step // 4 for step in range(5)]
    score(cuts[0], cuts[1])
    own_round(1, 2)
    score(cuts[1], cuts[4])
    lse_copies = spread(lse_all, lse_send, lse_recv)
    for distance in range(3, line):
        own_round(1, distance)
    other_round(1, 1)
    side_round(1, line - 1)
    collect(lse_all, lse_send, lse_recv)
    top = lse_all[0]
    for index in range(1, n_tile):
        top = jnp.maximum(top, lse_all[index])
    total = jnp.exp(lse_all[0] - top)
    for index in range(1, n_tile):
        total = total + jnp.exp(lse_all[index] - top)
    row_buf[...] = jnp.exp(max_buf[...] - (top + jnp.log(total)))

    @pl.loop(0, heads, unroll=2)
    def _(head):
        start = window(head)
        probs = expd[head] * row_buf[pl.ds(head, 1), :]
        expd[head] = probs
        value_grad[:, pl.ds(start, WIN)] += dot_nn(probs.astype(jnp.bfloat16), grad_win[head])

    for distance in range(2, line - 1):
        other_round(1, distance)
    close_round(1)

    values[...] = dot_nn(tiles[...], weights[1]).astype(jnp.bfloat16)

    for head in range(heads):
        part = dot_nn(values[:, fixed(head)], grad_turn[head])
        prob_grad[head] = part
        weighted_all[me, head : head + 1, :] = jnp.sum(expd[head] * part, axis=0, keepdims=True)

    sum_copies = spread(weighted_all, sum_send, sum_recv)

    value_cast = value_grad[...].astype(jnp.bfloat16)

    @pl.loop(0, 2 * chunks, unroll=2)
    def _(index):
        rows = pl.ds(pl.multiple_of(index * WIN, WIN), WIN)
        acc[index] = dot_nt(value_cast, weights[1, rows, :])

    collect(weighted_all, sum_send, sum_recv)
    delta = weighted_all[0]
    for index in range(1, n_tile):
        delta = delta + weighted_all[index]
    row_buf[...] = delta

    for head in range(heads):
        gap = prob_grad[head] - row_buf[head : head + 1, :]
        dscore = (inv_scale * expd[head] * gap).astype(jnp.bfloat16)
        key_grad[:, fixed(head)] += dot_nn(dscore, query_win[head])

    key_cast = key_grad[...].astype(jnp.bfloat16)

    def pair_copy(index):
        columns = pl.ds(index * WIN, WIN)
        return pltpu.make_async_remote_copy(
            src_ref=to_pair.at[:, columns],
            dst_ref=pair_ref.at[:, columns],
            send_sem=pair_send.at[index],
            recv_sem=pair_recv.at[index],
            device_id={"head": 1 - group},
            device_id_type=MESH,
        )

    def partial_sum(chunk):
        rows = pl.ds(pl.multiple_of(chunk * WIN, WIN), WIN)
        return (acc[chunk] + dot_nt(key_cast, weights[0, rows, :])).astype(jnp.bfloat16)

    for index in range(chunks):
        to_pair[:, index * WIN : (index + 1) * WIN] = partial_sum(chunks * (1 - group) + index)
        pair_copy(index).start()
    for index in range(chunks):
        own_ref[:, index * WIN : (index + 1) * WIN] = partial_sum(chunks * group + index)

    for index in range(chunks):
        pair_copy(index).wait_recv()
    for index in range(chunks):
        pair_copy(index).wait_send()
    for copy in lse_copies + sum_copies:
        copy.wait_send()
    assert len(started) <= SENDS
    for index, (cond, what) in enumerate(started):
        if cond is None:
            remote(index, *what).wait_send()
        else:
            pl.when(cond)(functools.partial(lambda i, w: remote(i, *w).wait_send(), index, what))


def fused_device(across, tiles_in, key_weight, value_weight, queries, out_grad, valid_count, tile_mask):
    n_tile = lax.axis_size("tile")
    tile_dev, depth = tiles_in.shape[1:]
    latents, width = queries.shape
    shard = key_weight.shape[0]
    heads = width // HDIM
    chunks = depth // 2 // WIN
    bf16, f32 = jnp.bfloat16, jnp.float32
    dma = pltpu.SemaphoreType.DMA
    own, pair = pl.pallas_call(
        functools.partial(fused, n_tile // across, across, shard, width, heads, chunks),
        out_shape=[jax.ShapeDtypeStruct((tile_dev, depth // 2), bf16)] * 2,
        in_specs=[pl.BlockSpec(memory_space=pl.ANY)] * 5
        + [pl.BlockSpec(memory_space=pltpu.SMEM), pl.BlockSpec(memory_space=pltpu.VMEM)],
        out_specs=[pl.BlockSpec(memory_space=pltpu.VMEM)] * 2,
        scratch_shapes=[
            pltpu.VMEM((2, depth, width), bf16),
            pltpu.VMEM((tile_dev, depth), bf16),
            pltpu.VMEM((latents, width), bf16),
            pltpu.VMEM((latents, width), bf16),
            pltpu.VMEM((heads, latents, WIN), bf16),
            pltpu.VMEM((heads, latents, WIN), bf16),
            pltpu.VMEM((heads, WIN, latents), bf16),
            pltpu.VMEM((heads, WIN, latents), bf16),
            pltpu.VMEM((3, tile_dev, width), bf16),
            pltpu.VMEM((tile_dev, width), bf16),
            pltpu.VMEM((heads, tile_dev, latents), f32),
            pltpu.VMEM((heads, tile_dev, latents), f32),
            pltpu.VMEM((heads, latents), f32),
            pltpu.VMEM((n_tile, heads, latents), f32),
            pltpu.VMEM((n_tile, heads, latents), f32),
            pltpu.VMEM((heads, latents), f32),
            pltpu.VMEM((tile_dev, width), f32),
            pltpu.VMEM((tile_dev, width), f32),
            pltpu.VMEM((2 * chunks, tile_dev, WIN), f32),
            pltpu.VMEM((tile_dev, chunks * WIN), bf16),
            pltpu.VMEM((tile_dev, 128), f32),
            dma((5,)),
            dma((SENDS,)),
            dma((2 * n_tile * 2 * SUBS,)),
            dma((n_tile,)),
            dma((n_tile,)),
            dma((n_tile,)),
            dma((n_tile,)),
            dma((chunks,)),
            dma((chunks,)),
        ],
        compiler_params=pltpu.CompilerParams(
            collective_id=0, has_side_effects=True, vmem_limit_bytes=56 * 2**20
        ),
        cost_estimate=pl.CostEstimate(
            flops=4 * tile_dev * depth * width * 2, bytes_accessed=8 * 2**20, transcendentals=2**20
        ),
    )(tiles_in, key_weight, value_weight, queries, out_grad, valid_count, tile_mask)
    return (own.astype(f32) + pair.astype(f32)).astype(bf16)[None]


def solution(mesh):
    across = mesh.shape["dp"]

    def device(tiles_in, key_weight, *rest):
        fits = (
            across == 2
            and mesh.shape["head"] == 2
            and mesh.shape["tile"] >= 3 * across
            and key_weight.shape[0] % (32 * SUBS) == 0
            and tiles_in.shape[2] % (2 * WIN) == 0
        )
        body = functools.partial(fused_device, across) if fits else per_device
        return body(tiles_in, key_weight, *rest)

    return jax.shard_map(
        device,
        mesh=mesh,
        in_specs=(
            P("dp", "tile", None),
            P("tile", "head"),
            P("tile", "head"),
            P(None, "head"),
            P("dp", None, "head"),
            P("dp"),
            P("dp", "tile"),
        ),
        out_specs=P("dp", "tile", "head"),
        check_vma=False,
    )
```

```python
import functools

import jax
import jax.numpy as jnp
from jax import lax
from jax.experimental import pallas as pl
from jax.experimental.pallas import tpu as pltpu
from jax.sharding import PartitionSpec as P

HDIM = 80


NEG_LARGE = -1e30
NEG_FLOOR = -1e29
WIN = 256
SUBS = 5
SENDS = 512
UP, DOWN, ACROSS, TWIN = range(4)
MESH = pl.DeviceIdType.MESH


def per_device(tiles_in, key_weight, value_weight, queries, out_grad, valid_count, tile_mask):
    inv_scale = HDIM ** (-0.5)
    tile_dev = tiles_in.shape[1]
    group_width = queries.shape[1]
    heads_here = group_width // HDIM
    latents = queries.shape[0]
    local_tiles = tiles_in[0]
    positions = lax.axis_index("tile") * tile_dev + jnp.arange(tile_dev, dtype=jnp.int32)
    kept = (tile_mask[0] == 1) | (positions == 0)
    valid = ((positions < valid_count[0]) & kept)[None, None, :]
    full_key, full_value = (
        lax.all_gather(key_weight, "tile", axis=0, tiled=True),
        lax.all_gather(value_weight, "tile", axis=0, tiled=True),
    )
    keys = jnp.dot(local_tiles, full_key, preferred_element_type=jnp.float32)
    values = jnp.dot(local_tiles, full_value, preferred_element_type=jnp.float32).astype(
        jnp.bfloat16
    )
    query_heads = queries.reshape(latents, heads_here, HDIM)
    query_wide = queries.astype(jnp.float32).reshape(latents, heads_here, HDIM)
    key_heads = keys.reshape(tile_dev, heads_here, HDIM)
    value_heads = values.reshape(tile_dev, heads_here, HDIM)
    grad_heads = out_grad[0].reshape(latents, heads_here, HDIM)
    scores = (
        jnp.einsum(
            "lhd,thd->hlt",
            query_wide,
            key_heads,
            precision=lax.Precision.HIGHEST,
            preferred_element_type=jnp.float32,
        )
        * inv_scale
    )
    prob_grad = jnp.einsum(
        "lhd,thd->hlt", grad_heads, value_heads, preferred_element_type=jnp.float32
    )
    local_max = jnp.max(jnp.where(valid, scores, NEG_LARGE), axis=2)
    row_max = lax.pmax(local_max, "tile")
    expd = jnp.where(valid, jnp.exp(scores - row_max[:, :, None]), 0.0)
    total, weighted = lax.psum((jnp.sum(expd, axis=2), jnp.sum(expd * prob_grad, axis=2)), "tile")
    delta = weighted / total
    probs = expd / total[:, :, None]
    dscore = (inv_scale * probs * (prob_grad - delta[:, :, None])).astype(jnp.bfloat16)
    value_grad = (
        jnp.einsum(
            "hlt,lhd->thd",
            probs.astype(jnp.bfloat16),
            grad_heads,
            preferred_element_type=jnp.float32,
        )
        .astype(jnp.bfloat16)
        .reshape(tile_dev, group_width)
    )
    key_grad = (
        jnp.einsum("hlt,lhd->thd", dscore, query_heads, preferred_element_type=jnp.float32)
        .astype(jnp.bfloat16)
        .reshape(tile_dev, group_width)
    )
    partial_sum = jnp.einsum("tc,rc->tr", key_grad, full_key, preferred_element_type=jnp.float32)
    partial_sum = partial_sum + jnp.einsum(
        "tc,rc->tr", value_grad, full_value, preferred_element_type=jnp.float32
    )
    rounded = partial_sum.astype(jnp.bfloat16)
    summed = lax.psum_scatter(rounded[None], "head", scatter_dimension=2, tiled=True).astype(
        jnp.float32
    )
    return summed.astype(jnp.bfloat16)


def dot_nt(a, b):
    return lax.dot_general(a, b, (((1,), (1,)), ((), ())), preferred_element_type=jnp.float32)


def dot_nn(a, b):
    return jnp.dot(a, b, preferred_element_type=jnp.float32)


def fused(
    line, across, shard, width, heads, chunks,
    tiles_hbm, key_hbm, value_hbm, query_hbm, grad_hbm, count_ref, mask_ref,
    own_ref, pair_ref,
    weights, tiles, query, grad, query_win, grad_win, query_turn, grad_turn, key_parts, values, expd, prob_grad,
    max_buf, lse_all, weighted_all, row_buf, value_grad, key_grad, acc, to_pair, valid,
    local_sem, send_sem, recv_sem, lse_send, lse_recv, sum_send, sum_recv, pair_send, pair_recv,
):
    n_tile = line * across
    half = shard // 2
    size = half // SUBS
    inv_scale = HDIM ** (-0.5)
    me = lax.axis_index("tile")
    slide = lax.axis_index("dp")
    group = lax.axis_index("head")
    z = me // across
    x = me % across
    beside = me + 1 - 2 * x
    twin = slide + 1 - 2 * (slide % 2)
    mine, other = slide % 2, 1 - slide % 2
    devices = {
        UP: {"tile": me + across},
        DOWN: {"tile": me - across},
        ACROSS: {"tile": beside},
        TWIN: {"dp": twin},
    }
    sources = (key_hbm, value_hbm)
    started = []

    def copy_in(src, dst, index):
        copy = pltpu.make_async_copy(src, dst, local_sem.at[index])
        copy.start()
        return copy

    own_rows = pl.ds(pl.multiple_of(me * shard, 16), shard)
    query_copy = copy_in(query_hbm, query, 0)
    grad_copy = copy_in(grad_hbm.at[0], grad, 1)
    tiles_copy = copy_in(tiles_hbm.at[0], tiles, 2)
    own_copies = [copy_in(sources[m], weights.at[m, own_rows], 3 + m) for m in range(2)]

    barrier = pltpu.get_barrier_semaphore()
    for step in range(1, n_tile):
        pl.semaphore_signal(
            barrier, inc=1, device_id={"tile": (me + step) % n_tile}, device_id_type=MESH
        )
    pl.semaphore_signal(barrier, inc=1, device_id={"dp": twin}, device_id_type=MESH)
    pl.semaphore_signal(barrier, inc=1, device_id={"head": 1 - group}, device_id_type=MESH)
    pl.semaphore_wait(barrier, n_tile + 1)

    def piece(m, owner, part, sub, way, first=False):
        offset = part * half + sub * size
        rows = pl.ds(pl.multiple_of(owner * shard + offset, 16), size)
        src = weights.at[m, rows]
        if first:
            src = sources[m].at[pl.ds(pl.multiple_of(offset, 16), size)]
        return src, weights.at[m, rows], ((m * n_tile + owner) * 2 + part) * SUBS + sub, devices[way]

    def remote(index, *what):
        src, dst, landing, device = piece(*what)
        return pltpu.make_async_remote_copy(
            src_ref=src,
            dst_ref=dst,
            send_sem=send_sem.at[index],
            recv_sem=recv_sem.at[landing],
            device_id=device,
            device_id_type=MESH,
        )

    def send(cond, *what):
        index = len(started)
        started.append((cond, what))
        if cond is None:
            remote(index, *what).start()
        else:
            pl.when(cond)(lambda: remote(index, *what).start())

    def arrive(cond, m, owner, part, sub):
        if cond is None:
            remote(0, m, owner, part, sub, ACROSS).wait_recv()
        else:
            pl.when(cond)(lambda: remote(0, m, owner, part, sub, ACROSS).wait_recv())

    def drain(m):
        assert len(started) <= SENDS
        for index, (cond, what) in enumerate(started):
            if what[0] != m:
                continue
            if cond is None:
                remote(index, *what).wait_send()
            else:
                pl.when(cond)(functools.partial(lambda i, w: remote(i, *w).wait_send(), index, what))

    def both(a, b):
        return b if a is None else (a if b is None else jnp.logical_and(a, b))

    can_up, can_down = z < line - 1, z > 0
    ways = ((UP, can_up), (DOWN, can_down))

    def held_at(base, distance):
        if distance == 0:
            return [(None, base)]
        return [
            (z >= distance, base - distance * across),
            (z + distance < line, base + distance * across),
        ]

    def open_own(m):
        for sub in range(SUBS):
            for way, can in ways:
                send(can, m, me, mine, sub, way, True)

    def open_side(m):
        for sub in range(SUBS):
            send(None, m, me, mine, sub, ACROSS, True)

    def side_round(m, distance):
        for sub in range(SUBS):
            for there, owner in held_at(beside, distance):
                arrive(there, m, owner, mine, sub)
                if distance > 0:
                    send(there, m, owner, mine, sub, TWIN)

    def own_round(m, distance):
        last = distance == line - 1
        for sub in range(SUBS):
            for (there, owner), (way, can) in zip(held_at(me, distance), ways):
                arrive(there, m, owner, mine, sub)
                if not last:
                    send(both(there, can), m, owner, mine, sub, way)
                send(there, m, owner, mine, sub, ACROSS)
                if last:
                    send(there, m, owner, mine, sub, TWIN)
        if last:
            for sub in range(SUBS):
                send(None, m, me, other, sub, ACROSS, True)
        for way, can, ends in ((UP, can_up, z), (DOWN, can_down, line - 1 - z)):
            turn = jnp.maximum(ends, 1) == distance
            for sub in range(SUBS):
                send(both(turn, can), m, me, other, sub, way, True)
        side_round(m, distance - 1)

    def other_round(m, distance):
        for sub in range(SUBS):
            for (there, owner), (way, can) in zip(held_at(me, distance), ways):
                arrive(there, m, owner, other, sub)
                if distance + 1 < line - 1:
                    send(both(there, can), m, owner, other, sub, way)

    def close_round(m):
        for sub in range(SUBS):
            for distance in range(line):
                for there, owner in held_at(beside, distance):
                    arrive(there, m, owner, other, sub)
            for there, owner in held_at(me, line - 1):
                arrive(there, m, owner, other, sub)

    def window(head):
        start = 128 * jnp.minimum((head * HDIM) // 128, (width - WIN) // 128)
        return pl.multiple_of(start, 128)

    def fixed(head):
        start = 128 * min((head * HDIM) // 128, (width - WIN) // 128)
        return slice(start, start + WIN)

    def spread(buffer, send_sems, recv_sems):
        copies = []
        for step in range(1, n_tile):
            copies.append(
                pltpu.make_async_remote_copy(
                    src_ref=buffer.at[me],
                    dst_ref=buffer.at[me],
                    send_sem=send_sems.at[step],
                    recv_sem=recv_sems.at[me],
                    device_id={"tile": (me + step) % n_tile},
                    device_id_type=MESH,
                )
            )
            copies[-1].start()
        return copies

    def collect(buffer, send_sems, recv_sems):
        for step in range(1, n_tile):
            owner = (me + n_tile - step) % n_tile
            pltpu.make_async_remote_copy(
                src_ref=buffer.at[owner],
                dst_ref=buffer.at[owner],
                send_sem=send_sems.at[step],
                recv_sem=recv_sems.at[owner],
                device_id={"tile": owner},
                device_id_type=MESH,
            ).wait_recv()

    open_own(0)
    open_side(0)

    positions = me * tiles.shape[0] + lax.broadcasted_iota(jnp.int32, (128, tiles.shape[0]), 1)
    kept = (mask_ref[...] == 1) | (positions == 0)
    valid[...] = jnp.where(kept & (positions < count_ref[0]), 1.0, 0.0).T

    query_copy.wait()
    grad_copy.wait()

    @pl.loop(0, heads)
    def _(head):
        start = window(head)
        column = start + lax.broadcasted_iota(jnp.int32, (query.shape[0], WIN), 1)
        inside = (column >= head * HDIM) & (column < (head + 1) * HDIM)
        for whole, cut, turn in ((query, query_win, query_turn), (grad, grad_win, grad_turn)):
            part = jnp.where(inside, whole[:, pl.ds(start, WIN)].astype(jnp.float32), 0.0)
            cut[head] = part.astype(jnp.bfloat16)
            turn[head] = part.T.astype(jnp.bfloat16)

    value_grad[...] = jnp.zeros_like(value_grad)
    key_grad[...] = jnp.zeros_like(key_grad)

    for distance in range(1, line):
        own_round(0, distance)
    open_side(1)
    other_round(0, 1)
    open_own(1)
    side_round(0, line - 1)
    for distance in range(2, line - 1):
        other_round(0, distance)
    own_round(1, 1)
    close_round(0)

    tiles_copy.wait()
    for copy in own_copies:
        copy.wait()
    keys = dot_nn(tiles[...], weights[0])
    for index in range(3):
        part = keys.astype(jnp.bfloat16)
        key_parts[index] = part
        keys = keys - part.astype(jnp.float32)

    def score(first, last):
        @pl.loop(first, last, unroll=2)
        def _(head):
            start = window(head)
            cut = query_turn[head]
            scores = dot_nn(key_parts[2, :, pl.ds(start, WIN)], cut)
            scores = scores + dot_nn(key_parts[1, :, pl.ds(start, WIN)], cut)
            scores = scores + dot_nn(key_parts[0, :, pl.ds(start, WIN)], cut)
            scores = jnp.where(valid[:, :1] > 0.0, scores * inv_scale, NEG_LARGE)
            row_max = jnp.maximum(jnp.max(scores, axis=0, keepdims=True), NEG_FLOOR)
            powers = jnp.exp(scores - row_max)
            total = jnp.sum(powers, axis=0, keepdims=True)
            expd[head] = powers
            max_buf[pl.ds(head, 1), :] = row_max
            lse_all[me, pl.ds(head, 1), :] = row_max + jnp.log(jnp.maximum(total, 1e-37))

    cuts = [heads * step // 4 for step in range(5)]
    score(cuts[0], cuts[1])
    own_round(1, 2)
    score(cuts[1], cuts[4])
    lse_copies = spread(lse_all, lse_send, lse_recv)
    for distance in range(3, line):
        own_round(1, distance)
    other_round(1, 1)
    side_round(1, line - 1)
    collect(lse_all, lse_send, lse_recv)
    top = lse_all[0]
    for index in range(1, n_tile):
        top = jnp.maximum(top, lse_all[index])
    total = jnp.exp(lse_all[0] - top)
    for index in range(1, n_tile):
        total = total + jnp.exp(lse_all[index] - top)
    row_buf[...] = jnp.exp(max_buf[...] - (top + jnp.log(total)))

    @pl.loop(0, heads, unroll=2)
    def _(head):
        start = window(head)
        probs = expd[head] * row_buf[pl.ds(head, 1), :]
        expd[head] = probs
        value_grad[:, pl.ds(start, WIN)] += dot_nn(probs.astype(jnp.bfloat16), grad_win[head])

    for distance in range(2, line - 1):
        other_round(1, distance)
    drain(0)
    close_round(1)

    values[...] = dot_nn(tiles[...], weights[1]).astype(jnp.bfloat16)

    for head in range(heads):
        part = dot_nn(values[:, fixed(head)], grad_turn[head])
        prob_grad[head] = part
        weighted_all[me, head : head + 1, :] = jnp.sum(expd[head] * part, axis=0, keepdims=True)

    sum_copies = spread(weighted_all, sum_send, sum_recv)
    drain(1)

    value_cast = value_grad[...].astype(jnp.bfloat16)

    @pl.loop(0, 2 * chunks, unroll=2)
    def _(index):
        rows = pl.ds(pl.multiple_of(index * WIN, WIN), WIN)
        acc[index] = dot_nt(value_cast, weights[1, rows, :])

    collect(weighted_all, sum_send, sum_recv)
    delta = weighted_all[0]
    for index in range(1, n_tile):
        delta = delta + weighted_all[index]
    row_buf[...] = delta

    for head in range(heads):
        gap = prob_grad[head] - row_buf[head : head + 1, :]
        dscore = (inv_scale * expd[head] * gap).astype(jnp.bfloat16)
        key_grad[:, fixed(head)] += dot_nn(dscore, query_win[head])

    key_cast = key_grad[...].astype(jnp.bfloat16)

    def pair_copy(index):
        columns = pl.ds(index * WIN, WIN)
        return pltpu.make_async_remote_copy(
            src_ref=to_pair.at[:, columns],
            dst_ref=pair_ref.at[:, columns],
            send_sem=pair_send.at[index],
            recv_sem=pair_recv.at[index],
            device_id={"head": 1 - group},
            device_id_type=MESH,
        )

    def partial_sum(chunk):
        rows = pl.ds(pl.multiple_of(chunk * WIN, WIN), WIN)
        return (acc[chunk] + dot_nt(key_cast, weights[0, rows, :])).astype(jnp.bfloat16)

    for index in range(chunks):
        to_pair[:, index * WIN : (index + 1) * WIN] = partial_sum(chunks * (1 - group) + index)
        pair_copy(index).start()
    for index in range(chunks):
        own_ref[:, index * WIN : (index + 1) * WIN] = partial_sum(chunks * group + index)

    for index in range(chunks):
        pair_copy(index).wait_recv()
    for index in range(chunks):
        pair_copy(index).wait_send()
    for copy in lse_copies + sum_copies:
        copy.wait_send()


def fused_device(across, tiles_in, key_weight, value_weight, queries, out_grad, valid_count, tile_mask):
    n_tile = lax.axis_size("tile")
    tile_dev, depth = tiles_in.shape[1:]
    latents, width = queries.shape
    shard = key_weight.shape[0]
    heads = width // HDIM
    chunks = depth // 2 // WIN
    bf16, f32 = jnp.bfloat16, jnp.float32
    dma = pltpu.SemaphoreType.DMA
    own, pair = pl.pallas_call(
        functools.partial(fused, n_tile // across, across, shard, width, heads, chunks),
        out_shape=[jax.ShapeDtypeStruct((tile_dev, depth // 2), bf16)] * 2,
        in_specs=[pl.BlockSpec(memory_space=pl.ANY)] * 5
        + [pl.BlockSpec(memory_space=pltpu.SMEM), pl.BlockSpec(memory_space=pltpu.VMEM)],
        out_specs=[pl.BlockSpec(memory_space=pltpu.VMEM)] * 2,
        scratch_shapes=[
            pltpu.VMEM((2, depth, width), bf16),
            pltpu.VMEM((tile_dev, depth), bf16),
            pltpu.VMEM((latents, width), bf16),
            pltpu.VMEM((latents, width), bf16),
            pltpu.VMEM((heads, latents, WIN), bf16),
            pltpu.VMEM((heads, latents, WIN), bf16),
            pltpu.VMEM((heads, WIN, latents), bf16),
            pltpu.VMEM((heads, WIN, latents), bf16),
            pltpu.VMEM((3, tile_dev, width), bf16),
            pltpu.VMEM((tile_dev, width), bf16),
            pltpu.VMEM((heads, tile_dev, latents), f32),
            pltpu.VMEM((heads, tile_dev, latents), f32),
            pltpu.VMEM((heads, latents), f32),
            pltpu.VMEM((n_tile, heads, latents), f32),
            pltpu.VMEM((n_tile, heads, latents), f32),
            pltpu.VMEM((heads, latents), f32),
            pltpu.VMEM((tile_dev, width), f32),
            pltpu.VMEM((tile_dev, width), f32),
            pltpu.VMEM((2 * chunks, tile_dev, WIN), f32),
            pltpu.VMEM((tile_dev, chunks * WIN), bf16),
            pltpu.VMEM((tile_dev, 128), f32),
            dma((5,)),
            dma((SENDS,)),
            dma((2 * n_tile * 2 * SUBS,)),
            dma((n_tile,)),
            dma((n_tile,)),
            dma((n_tile,)),
            dma((n_tile,)),
            dma((chunks,)),
            dma((chunks,)),
        ],
        compiler_params=pltpu.CompilerParams(
            collective_id=0, has_side_effects=True, vmem_limit_bytes=56 * 2**20
        ),
        cost_estimate=pl.CostEstimate(
            flops=4 * tile_dev * depth * width * 2, bytes_accessed=8 * 2**20, transcendentals=2**20
        ),
    )(tiles_in, key_weight, value_weight, queries, out_grad, valid_count, tile_mask)
    return (own.astype(f32) + pair.astype(f32)).astype(bf16)[None]


def solution(mesh):
    across = mesh.shape["dp"]

    def device(tiles_in, key_weight, *rest):
        fits = (
            across == 2
            and mesh.shape["head"] == 2
            and mesh.shape["tile"] >= 3 * across
            and key_weight.shape[0] % (32 * SUBS) == 0
            and tiles_in.shape[2] % (2 * WIN) == 0
        )
        body = functools.partial(fused_device, across) if fits else per_device
        return body(tiles_in, key_weight, *rest)

    return jax.shard_map(
        device,
        mesh=mesh,
        in_specs=(
            P("dp", "tile", None),
            P("tile", "head"),
            P("tile", "head"),
            P(None, "head"),
            P("dp", None, "head"),
            P("dp"),
            P("dp", "tile"),
        ),
        out_specs=P("dp", "tile", "head"),
        check_vma=False,
    )
```

```python
import functools

import jax
import jax.numpy as jnp
from jax import lax
from jax.experimental import pallas as pl
from jax.experimental.pallas import tpu as pltpu
from jax.sharding import PartitionSpec as P

HDIM = 80


NEG_LARGE = -1e30
NEG_FLOOR = -1e29
WIN = 256
SUBS = 2
SENDS = 192
UP, DOWN, ACROSS, TWIN = range(4)
MESH = pl.DeviceIdType.MESH


def per_device(tiles_in, key_weight, value_weight, queries, out_grad, valid_count, tile_mask):
    inv_scale = HDIM ** (-0.5)
    tile_dev = tiles_in.shape[1]
    group_width = queries.shape[1]
    heads_here = group_width // HDIM
    latents = queries.shape[0]
    local_tiles = tiles_in[0]
    positions = lax.axis_index("tile") * tile_dev + jnp.arange(tile_dev, dtype=jnp.int32)
    kept = (tile_mask[0] == 1) | (positions == 0)
    valid = ((positions < valid_count[0]) & kept)[None, None, :]
    full_key, full_value = (
        lax.all_gather(key_weight, "tile", axis=0, tiled=True),
        lax.all_gather(value_weight, "tile", axis=0, tiled=True),
    )
    keys = jnp.dot(local_tiles, full_key, preferred_element_type=jnp.float32)
    values = jnp.dot(local_tiles, full_value, preferred_element_type=jnp.float32).astype(
        jnp.bfloat16
    )
    query_heads = queries.reshape(latents, heads_here, HDIM)
    query_wide = queries.astype(jnp.float32).reshape(latents, heads_here, HDIM)
    key_heads = keys.reshape(tile_dev, heads_here, HDIM)
    value_heads = values.reshape(tile_dev, heads_here, HDIM)
    grad_heads = out_grad[0].reshape(latents, heads_here, HDIM)
    scores = (
        jnp.einsum(
            "lhd,thd->hlt",
            query_wide,
            key_heads,
            precision=lax.Precision.HIGHEST,
            preferred_element_type=jnp.float32,
        )
        * inv_scale
    )
    prob_grad = jnp.einsum(
        "lhd,thd->hlt", grad_heads, value_heads, preferred_element_type=jnp.float32
    )
    local_max = jnp.max(jnp.where(valid, scores, NEG_LARGE), axis=2)
    row_max = lax.pmax(local_max, "tile")
    expd = jnp.where(valid, jnp.exp(scores - row_max[:, :, None]), 0.0)
    total, weighted = lax.psum((jnp.sum(expd, axis=2), jnp.sum(expd * prob_grad, axis=2)), "tile")
    delta = weighted / total
    probs = expd / total[:, :, None]
    dscore = (inv_scale * probs * (prob_grad - delta[:, :, None])).astype(jnp.bfloat16)
    value_grad = (
        jnp.einsum(
            "hlt,lhd->thd",
            probs.astype(jnp.bfloat16),
            grad_heads,
            preferred_element_type=jnp.float32,
        )
        .astype(jnp.bfloat16)
        .reshape(tile_dev, group_width)
    )
    key_grad = (
        jnp.einsum("hlt,lhd->thd", dscore, query_heads, preferred_element_type=jnp.float32)
        .astype(jnp.bfloat16)
        .reshape(tile_dev, group_width)
    )
    partial_sum = jnp.einsum("tc,rc->tr", key_grad, full_key, preferred_element_type=jnp.float32)
    partial_sum = partial_sum + jnp.einsum(
        "tc,rc->tr", value_grad, full_value, preferred_element_type=jnp.float32
    )
    rounded = partial_sum.astype(jnp.bfloat16)
    summed = lax.psum_scatter(rounded[None], "head", scatter_dimension=2, tiled=True).astype(
        jnp.float32
    )
    return summed.astype(jnp.bfloat16)


def dot_nt(a, b):
    return lax.dot_general(a, b, (((1,), (1,)), ((), ())), preferred_element_type=jnp.float32)


def dot_nn(a, b):
    return jnp.dot(a, b, preferred_element_type=jnp.float32)


def fused(
    line, across, shard, width, heads, chunks,
    tiles_hbm, key_hbm, value_hbm, query_hbm, grad_hbm, count_ref, mask_ref,
    own_ref, pair_ref,
    weights, tiles, query, grad, query_win, grad_win, query_turn, grad_turn, key_parts, values, expd, prob_grad,
    max_buf, lse_all, weighted_all, row_buf, value_grad, key_grad, acc, to_pair, valid,
    local_sem, send_sem, recv_sem, lse_send, lse_recv, sum_send, sum_recv, pair_send, pair_recv,
):
    n_tile = line * across
    half = shard // 2
    size = half // SUBS
    inv_scale = HDIM ** (-0.5)
    me = lax.axis_index("tile")
    slide = lax.axis_index("dp")
    group = lax.axis_index("head")
    z = me // across
    x = me % across
    beside = me + 1 - 2 * x
    twin = slide + 1 - 2 * (slide % 2)
    mine, other = slide % 2, 1 - slide % 2
    devices = {
        UP: {"tile": me + across},
        DOWN: {"tile": me - across},
        ACROSS: {"tile": beside},
        TWIN: {"dp": twin},
    }
    sources = (key_hbm, value_hbm)
    started = []

    def copy_in(src, dst, index):
        copy = pltpu.make_async_copy(src, dst, local_sem.at[index])
        copy.start()
        return copy

    own_rows = pl.ds(pl.multiple_of(me * shard, 16), shard)
    query_copy = copy_in(query_hbm, query, 0)
    grad_copy = copy_in(grad_hbm.at[0], grad, 1)
    tiles_copy = copy_in(tiles_hbm.at[0], tiles, 2)
    own_copies = [copy_in(sources[m], weights.at[m, own_rows], 3 + m) for m in range(2)]

    barrier = pltpu.get_barrier_semaphore()
    for step in range(1, n_tile):
        pl.semaphore_signal(
            barrier, inc=1, device_id={"tile": (me + step) % n_tile}, device_id_type=MESH
        )
    pl.semaphore_signal(barrier, inc=1, device_id={"dp": twin}, device_id_type=MESH)
    pl.semaphore_signal(barrier, inc=1, device_id={"head": 1 - group}, device_id_type=MESH)
    pl.semaphore_wait(barrier, n_tile + 1)

    def piece(m, owner, part, sub, way, first=False):
        offset = part * half + sub * size
        rows = pl.ds(pl.multiple_of(owner * shard + offset, 16), size)
        src = weights.at[m, rows]
        if first:
            src = sources[m].at[pl.ds(pl.multiple_of(offset, 16), size)]
        return src, weights.at[m, rows], ((m * n_tile + owner) * 2 + part) * SUBS + sub, devices[way]

    def remote(index, *what):
        src, dst, landing, device = piece(*what)
        return pltpu.make_async_remote_copy(
            src_ref=src,
            dst_ref=dst,
            send_sem=send_sem.at[index],
            recv_sem=recv_sem.at[landing],
            device_id=device,
            device_id_type=MESH,
        )

    def send(cond, *what):
        index = len(started)
        started.append((cond, what))
        if cond is None:
            remote(index, *what).start()
        else:
            pl.when(cond)(lambda: remote(index, *what).start())

    def arrive(cond, m, owner, part, sub):
        if cond is None:
            remote(0, m, owner, part, sub, ACROSS).wait_recv()
        else:
            pl.when(cond)(lambda: remote(0, m, owner, part, sub, ACROSS).wait_recv())

    def drain(m):
        assert len(started) <= SENDS
        for index, (cond, what) in enumerate(started):
            if what[0] != m:
                continue
            if cond is None:
                remote(index, *what).wait_send()
            else:
                pl.when(cond)(functools.partial(lambda i, w: remote(i, *w).wait_send(), index, what))

    def both(a, b):
        return b if a is None else (a if b is None else jnp.logical_and(a, b))

    can_up, can_down = z < line - 1, z > 0
    ways = ((UP, can_up), (DOWN, can_down))

    def held_at(base, distance):
        if distance == 0:
            return [(None, base)]
        return [
            (z >= distance, base - distance * across),
            (z + distance < line, base + distance * across),
        ]

    def open_own(m):
        for sub in range(SUBS):
            for way, can in ways:
                send(can, m, me, mine, sub, way, True)

    def open_side(m):
        for sub in range(SUBS):
            send(None, m, me, mine, sub, ACROSS, True)

    def side_round(m, distance):
        for sub in range(SUBS):
            for there, owner in held_at(beside, distance):
                arrive(there, m, owner, mine, sub)
                if distance > 0:
                    send(there, m, owner, mine, sub, TWIN)

    def own_round(m, distance):
        last = distance == line - 1
        for sub in range(SUBS):
            for (there, owner), (way, can) in zip(held_at(me, distance), ways):
                arrive(there, m, owner, mine, sub)
                if not last:
                    send(both(there, can), m, owner, mine, sub, way)
                send(there, m, owner, mine, sub, ACROSS)
                if last:
                    send(there, m, owner, mine, sub, TWIN)
        if last:
            for sub in range(SUBS):
                send(None, m, me, other, sub, ACROSS, True)
        for way, can, ends in ((UP, can_up, z), (DOWN, can_down, line - 1 - z)):
            turn = jnp.maximum(ends, 1) == distance
            for sub in range(SUBS):
                send(both(turn, can), m, me, other, sub, way, True)
        side_round(m, distance - 1)

    def other_round(m, distance):
        for sub in range(SUBS):
            for (there, owner), (way, can) in zip(held_at(me, distance), ways):
                arrive(there, m, owner, other, sub)
                if distance + 1 < line - 1:
                    send(both(there, can), m, owner, other, sub, way)

    def close_round(m):
        for sub in range(SUBS):
            for distance in range(line):
                for there, owner in held_at(beside, distance):
                    arrive(there, m, owner, other, sub)
            for there, owner in held_at(me, line - 1):
                arrive(there, m, owner, other, sub)

    def window(head):
        start = 128 * jnp.minimum((head * HDIM) // 128, (width - WIN) // 128)
        return pl.multiple_of(start, 128)

    def fixed(head):
        start = 128 * min((head * HDIM) // 128, (width - WIN) // 128)
        return slice(start, start + WIN)

    def spread(buffer, send_sems, recv_sems):
        copies = []
        for step in range(1, n_tile):
            copies.append(
                pltpu.make_async_remote_copy(
                    src_ref=buffer.at[me],
                    dst_ref=buffer.at[me],
                    send_sem=send_sems.at[step],
                    recv_sem=recv_sems.at[me],
                    device_id={"tile": (me + step) % n_tile},
                    device_id_type=MESH,
                )
            )
            copies[-1].start()
        return copies

    def collect(buffer, send_sems, recv_sems):
        for step in range(1, n_tile):
            owner = (me + n_tile - step) % n_tile
            pltpu.make_async_remote_copy(
                src_ref=buffer.at[owner],
                dst_ref=buffer.at[owner],
                send_sem=send_sems.at[step],
                recv_sem=recv_sems.at[owner],
                device_id={"tile": owner},
                device_id_type=MESH,
            ).wait_recv()

    open_own(0)
    open_side(0)

    positions = me * tiles.shape[0] + lax.broadcasted_iota(jnp.int32, (128, tiles.shape[0]), 1)
    kept = (mask_ref[...] == 1) | (positions == 0)
    valid[...] = jnp.where(kept & (positions < count_ref[0]), 1.0, 0.0).T

    query_copy.wait()
    grad_copy.wait()

    @pl.loop(0, heads)
    def _(head):
        start = window(head)
        column = start + lax.broadcasted_iota(jnp.int32, (query.shape[0], WIN), 1)
        inside = (column >= head * HDIM) & (column < (head + 1) * HDIM)
        for whole, cut, turn in ((query, query_win, query_turn), (grad, grad_win, grad_turn)):
            part = jnp.where(inside, whole[:, pl.ds(start, WIN)].astype(jnp.float32), 0.0)
            cut[head] = part.astype(jnp.bfloat16)
            turn[head] = part.T.astype(jnp.bfloat16)

    value_grad[...] = jnp.zeros_like(value_grad)
    key_grad[...] = jnp.zeros_like(key_grad)

    for distance in range(1, line):
        own_round(0, distance)
    open_side(1)
    other_round(0, 1)
    open_own(1)
    side_round(0, line - 1)
    for distance in range(2, line - 1):
        other_round(0, distance)
    own_round(1, 1)
    close_round(0)

    tiles_copy.wait()
    for copy in own_copies:
        copy.wait()
    keys = dot_nn(tiles[...], weights[0])
    for index in range(3):
        part = keys.astype(jnp.bfloat16)
        key_parts[index] = part
        keys = keys - part.astype(jnp.float32)

    def score(first, last):
        @pl.loop(first, last, unroll=2)
        def _(head):
            start = window(head)
            cut = query_turn[head]
            scores = dot_nn(key_parts[2, :, pl.ds(start, WIN)], cut)
            scores = scores + dot_nn(key_parts[1, :, pl.ds(start, WIN)], cut)
            scores = scores + dot_nn(key_parts[0, :, pl.ds(start, WIN)], cut)
            scores = jnp.where(valid[:, :1] > 0.0, scores * inv_scale, NEG_LARGE)
            row_max = jnp.maximum(jnp.max(scores, axis=0, keepdims=True), NEG_FLOOR)
            powers = jnp.exp(scores - row_max)
            total = jnp.sum(powers, axis=0, keepdims=True)
            expd[head] = powers
            max_buf[pl.ds(head, 1), :] = row_max
            lse_all[me, pl.ds(head, 1), :] = row_max + jnp.log(jnp.maximum(total, 1e-37))

    cuts = [heads * step // 4 for step in range(5)]
    score(cuts[0], cuts[1])
    own_round(1, 2)
    score(cuts[1], cuts[2])
    for distance in range(3, line):
        own_round(1, distance)
    score(cuts[2], cuts[4])
    lse_copies = spread(lse_all, lse_send, lse_recv)
    other_round(1, 1)
    side_round(1, line - 1)
    collect(lse_all, lse_send, lse_recv)
    top = lse_all[0]
    for index in range(1, n_tile):
        top = jnp.maximum(top, lse_all[index])
    total = jnp.exp(lse_all[0] - top)
    for index in range(1, n_tile):
        total = total + jnp.exp(lse_all[index] - top)
    row_buf[...] = jnp.exp(max_buf[...] - (top + jnp.log(total)))

    @pl.loop(0, heads, unroll=2)
    def _(head):
        start = window(head)
        probs = expd[head] * row_buf[pl.ds(head, 1), :]
        expd[head] = probs
        value_grad[:, pl.ds(start, WIN)] += dot_nn(probs.astype(jnp.bfloat16), grad_win[head])

    for distance in range(2, line - 1):
        other_round(1, distance)
    drain(0)
    close_round(1)

    values[...] = dot_nn(tiles[...], weights[1]).astype(jnp.bfloat16)

    for head in range(heads):
        part = dot_nn(values[:, fixed(head)], grad_turn[head])
        prob_grad[head] = part
        weighted_all[me, head : head + 1, :] = jnp.sum(expd[head] * part, axis=0, keepdims=True)

    sum_copies = spread(weighted_all, sum_send, sum_recv)
    drain(1)

    value_cast = value_grad[...].astype(jnp.bfloat16)

    @pl.loop(0, 2 * chunks, unroll=2)
    def _(index):
        rows = pl.ds(pl.multiple_of(index * WIN, WIN), WIN)
        acc[index] = dot_nt(value_cast, weights[1, rows, :])

    collect(weighted_all, sum_send, sum_recv)
    delta = weighted_all[0]
    for index in range(1, n_tile):
        delta = delta + weighted_all[index]
    row_buf[...] = delta

    for head in range(heads):
        gap = prob_grad[head] - row_buf[head : head + 1, :]
        dscore = (inv_scale * expd[head] * gap).astype(jnp.bfloat16)
        key_grad[:, fixed(head)] += dot_nn(dscore, query_win[head])

    key_cast = key_grad[...].astype(jnp.bfloat16)

    def pair_copy(index):
        columns = pl.ds(index * WIN, WIN)
        return pltpu.make_async_remote_copy(
            src_ref=to_pair.at[:, columns],
            dst_ref=pair_ref.at[:, columns],
            send_sem=pair_send.at[index],
            recv_sem=pair_recv.at[index],
            device_id={"head": 1 - group},
            device_id_type=MESH,
        )

    def partial_sum(chunk):
        rows = pl.ds(pl.multiple_of(chunk * WIN, WIN), WIN)
        return (acc[chunk] + dot_nt(key_cast, weights[0, rows, :])).astype(jnp.bfloat16)

    for index in range(chunks):
        to_pair[:, index * WIN : (index + 1) * WIN] = partial_sum(chunks * (1 - group) + index)
        pair_copy(index).start()
    for index in range(chunks):
        own_ref[:, index * WIN : (index + 1) * WIN] = partial_sum(chunks * group + index)

    for index in range(chunks):
        pair_copy(index).wait_recv()
    for index in range(chunks):
        pair_copy(index).wait_send()
    for copy in lse_copies + sum_copies:
        copy.wait_send()


def fused_device(across, tiles_in, key_weight, value_weight, queries, out_grad, valid_count, tile_mask):
    n_tile = lax.axis_size("tile")
    tile_dev, depth = tiles_in.shape[1:]
    latents, width = queries.shape
    shard = key_weight.shape[0]
    heads = width // HDIM
    chunks = depth // 2 // WIN
    bf16, f32 = jnp.bfloat16, jnp.float32
    dma = pltpu.SemaphoreType.DMA
    own, pair = pl.pallas_call(
        functools.partial(fused, n_tile // across, across, shard, width, heads, chunks),
        out_shape=[jax.ShapeDtypeStruct((tile_dev, depth // 2), bf16)] * 2,
        in_specs=[pl.BlockSpec(memory_space=pl.ANY)] * 5
        + [pl.BlockSpec(memory_space=pltpu.SMEM), pl.BlockSpec(memory_space=pltpu.VMEM)],
        out_specs=[pl.BlockSpec(memory_space=pltpu.VMEM)] * 2,
        scratch_shapes=[
            pltpu.VMEM((2, depth, width), bf16),
            pltpu.VMEM((tile_dev, depth), bf16),
            pltpu.VMEM((latents, width), bf16),
            pltpu.VMEM((latents, width), bf16),
            pltpu.VMEM((heads, latents, WIN), bf16),
            pltpu.VMEM((heads, latents, WIN), bf16),
            pltpu.VMEM((heads, WIN, latents), bf16),
            pltpu.VMEM((heads, WIN, latents), bf16),
            pltpu.VMEM((3, tile_dev, width), bf16),
            pltpu.VMEM((tile_dev, width), bf16),
            pltpu.VMEM((heads, tile_dev, latents), f32),
            pltpu.VMEM((heads, tile_dev, latents), f32),
            pltpu.VMEM((heads, latents), f32),
            pltpu.VMEM((n_tile, heads, latents), f32),
            pltpu.VMEM((n_tile, heads, latents), f32),
            pltpu.VMEM((heads, latents), f32),
            pltpu.VMEM((tile_dev, width), f32),
            pltpu.VMEM((tile_dev, width), f32),
            pltpu.VMEM((2 * chunks, tile_dev, WIN), f32),
            pltpu.VMEM((tile_dev, chunks * WIN), bf16),
            pltpu.VMEM((tile_dev, 128), f32),
            dma((5,)),
            dma((SENDS,)),
            dma((2 * n_tile * 2 * SUBS,)),
            dma((n_tile,)),
            dma((n_tile,)),
            dma((n_tile,)),
            dma((n_tile,)),
            dma((chunks,)),
            dma((chunks,)),
        ],
        compiler_params=pltpu.CompilerParams(
            collective_id=0, has_side_effects=True, vmem_limit_bytes=56 * 2**20
        ),
        cost_estimate=pl.CostEstimate(
            flops=4 * tile_dev * depth * width * 2, bytes_accessed=8 * 2**20, transcendentals=2**20
        ),
    )(tiles_in, key_weight, value_weight, queries, out_grad, valid_count, tile_mask)
    return (own.astype(f32) + pair.astype(f32)).astype(bf16)[None]


def solution(mesh):
    across = mesh.shape["dp"]

    def device(tiles_in, key_weight, *rest):
        fits = (
            across == 2
            and mesh.shape["head"] == 2
            and mesh.shape["tile"] >= 3 * across
            and key_weight.shape[0] % (32 * SUBS) == 0
            and tiles_in.shape[2] % (2 * WIN) == 0
        )
        body = functools.partial(fused_device, across) if fits else per_device
        return body(tiles_in, key_weight, *rest)

    return jax.shard_map(
        device,
        mesh=mesh,
        in_specs=(
            P("dp", "tile", None),
            P("tile", "head"),
            P("tile", "head"),
            P(None, "head"),
            P("dp", None, "head"),
            P("dp"),
            P("dp", "tile"),
        ),
        out_specs=P("dp", "tile", "head"),
        check_vma=False,
    )
```
